32 devices in a mesh: seq: 16 (over z, x, core), wt: 2 (over y).
Axes of the slice: x: 2, y: 2, z: 4, core: 2. Of those that a mesh axis runs over, the one named last changes fastest.
Arguments:
- tokens: bfloat16 [2, 2048, 1600], P('wt', 'seq'), may hold values from -6 to 6
- segment_ids: int32 [2, 2048], P('wt'), may hold values from 0 to 2, as said below
- cotangent: bfloat16 [2, 2048, 1600], P('wt', 'seq'), may hold values from -6 to 6
- norm_gain: float32 [1600], replicated, may hold values from 0.5 to 1.5
- query_weight: bfloat16 [1600, 1600], P(None, 'wt'), may hold values from -0.15625 to 0.15625
- key_weight: bfloat16 [1600, 320], P(None, 'wt'), may hold values from -0.15625 to 0.15625
- value_weight: bfloat16 [1600, 320], P(None, 'wt'), may hold values from -0.15625 to 0.15625
- head_weight: bfloat16 [1600, 1600], P(None, 'wt'), may hold values from -0.15625 to 0.15625
- input_weight: bfloat16 [1600, 6400], P(None, 'wt'), may hold values from -0.15625 to 0.15625
- filter_weight: float32 [4, 3200], replicated, may hold values from -3 to 3
- filter_bias: float32 [3200], replicated, may hold values from -3 to 3
- select_weight: bfloat16 [3200, 132], P(None, 'wt'), may hold values from -0.109375 to 0.109375
- step_weight: bfloat16 [3200, 100], P(None, 'wt'), may hold values from -0.625 to 0.625
- step_offset: float32 [3200], replicated, may hold values from -4 to -2
- decay_log: float32 [16, 3200], replicated, may hold values from -11 to 1
- direct_skip_weight: float32 [3200], replicated, may hold values from 0.5 to 1.5
- mixer_weight: bfloat16 [3200, 1600], P(None, 'wt'), may hold values from -0.109375 to 0.109375
- attend_gain: float32 [1600], replicated, may hold values from 0.5 to 1.5
- state_gain: float32 [1600], replicated, may hold values from 0.5 to 1.5
- feed_gain: float32 [1600], replicated, may hold values from 0.5 to 1.5
- gate_weight: bfloat16 [1600, 5504], P(None, 'wt'), may hold values from -0.15625 to 0.15625
- up_weight: bfloat16 [1600, 5504], P(None, 'wt'), may hold values from -0.15625 to 0.15625
- down_weight: bfloat16 [1600, 5504], P(None, 'wt'), may hold values from -0.078125 to 0.078125
Outputs:
- result: bfloat16 [2, 2048, 1600], P('wt', 'seq')
- tokens_gradient: float32 [2, 2048, 1600], P('wt', 'seq')
- norm_gradient: float32 [1600], replicated
- query_gradient: float32 [1600, 1600], P('seq', 'wt')
- key_gradient: float32 [1600, 320], P('seq', 'wt')
- value_gradient: float32 [1600, 320], P('seq', 'wt')
- head_gradient: float32 [1600, 1600], P('seq', 'wt')
- input_gradient: float32 [1600, 6400], P('seq', 'wt')
- filter_gradient: float32 [4, 3200], replicated
- bias_gradient: float32 [3200], replicated
- select_gradient: float32 [3200, 132], P('seq', 'wt')
- step_gradient: float32 [3200, 100], P('seq', 'wt')
- offset_gradient: float32 [3200], replicated
- decay_gradient: float32 [16, 3200], replicated
- skip_gradient: float32 [3200], replicated
- mixer_gradient: float32 [3200, 1600], P('seq', 'wt')
- attend_gradient: float32 [1600], replicated
- state_gradient: float32 [1600], replicated
- feed_gradient: float32 [1600], replicated
- gate_gradient: float32 [1600, 5504], P('seq', 'wt')
- up_gradient: float32 [1600, 5504], P('seq', 'wt')
- down_gradient: float32 [1600, 5504], P('seq', 'wt')
The draws below stay inside these ranges and needn't reach their ends.
Inputs may be any that keep to these rules, and one draw needn't show every extreme that they name: `segment_ids`: along each sequence the ids never fall: document 0 ends within the first 128 tokens, document 2 begins within the last 128 tokens, and document 1 lies between.
All inputs are finite; a program needn't handle non-finite values.
Results may differ from the reference program's by a relative error of at most 0.015.
The reference program's roundings to bfloat16 on the way count: a program that leaves them out, or rounds other values in their place, can miss the bound.
Values may be sent and summed in bfloat16 or wider, within the bound.
A program may use at most 768 MiB of HBM per device.

```python
import jax
import jax.numpy as jnp
from jax import lax

D = 1600
HEADS = 25
KEY_HEADS = 5
HEAD_SIZE = 64
INNER = 3200
STATE = 16
RANK = 100
KERNEL = 4
FF = 5504
WINDOW = 1024
TOK_DEV = 128
STRETCH = 128
QUERY_BLOCK = 512
SEQS = 2
LEN = 2048


def draw_segment_ids(key, part):
    key = jax.random.fold_in(key, 11)
    first_key, last_key = jax.random.split(key)
    first = jax.random.randint(first_key, (SEQS, 1), 1, TOK_DEV)
    last = jax.random.randint(last_key, (SEQS, 1), LEN - TOK_DEV + 1, LEN)
    places = jnp.arange(LEN, dtype=jnp.int32)[None, :]
    return (places >= first).astype(jnp.int32) + (places >= last).astype(jnp.int32)


def shard_levels(own_key, dims, shards, low, top_value):
    def one(axis_at, shards_of):
        draws = jax.random.uniform(jax.random.fold_in(jax.random.fold_in(own_key, 6), axis_at), (shards_of,), jnp.float32, low / len(shards), top_value / len(shards))
        return jnp.repeat(jnp.exp(draws), dims[axis_at] // shards_of).reshape((-1,) + (1,) * (len(dims) - axis_at - 1))

    level = one(*shards[0])
    for cut in shards[1:]:
        level = level * one(*cut)
    return level


def gaussian(own_key, shape, deviation, most, shards=(), kind=jnp.bfloat16):
    factor_of = shard_levels(own_key, shape, shards, -0.22, 0.18) if shards else 1.0
    values = jax.random.normal(own_key, shape, jnp.float32) * deviation * factor_of
    return jnp.minimum(jnp.maximum(values, -most), most).astype(kind)


def setup_inputs(seed: int = 0) -> dict:
    seeds = jax.random.split(jax.random.key(seed), 24)
    tokens = gaussian(seeds[0], (SEQS, LEN, D), 1.0, 6.0, ((0, 2), (1, 16)))
    segment_ids = draw_segment_ids(jax.random.fold_in(seeds[23], 71), 0)
    cotangent = gaussian(seeds[2], (SEQS, LEN, D), 1.0, 6.0, ((0, 2), (1, 16)))
    norm_gain = jnp.clip(1.0 + 0.1 * jax.random.normal(seeds[3], (D,), jnp.float32), 0.5, 1.5)
    query_weight = gaussian(seeds[4], (D, D), D ** -0.5, 0.15625, ((1, 2),))
    key_weight = gaussian(seeds[5], (D, KEY_HEADS * HEAD_SIZE), D ** -0.5, 0.15625, ((1, 2),))
    value_weight = gaussian(seeds[6], (D, KEY_HEADS * HEAD_SIZE), D ** -0.5, 0.15625, ((1, 2),))
    head_weight = gaussian(seeds[7], (D, D), D ** -0.5, 0.15625, ((1, 2),))
    input_weight = gaussian(seeds[8], (D, 2 * INNER), D ** -0.5, 0.15625, ((1, 2),))
    filter_weight = gaussian(seeds[9], (KERNEL, INNER), 0.5, 3.0, (), jnp.float32)
    filter_bias = gaussian(seeds[10], (INNER,), 0.5, 3.0, (), jnp.float32)
    select_weight = gaussian(seeds[11], (INNER, RANK + 2 * STATE), INNER ** -0.5, 0.109375, ((1, 2),))
    step_weight = gaussian(seeds[12], (INNER, RANK), RANK ** -0.5, 0.625, ((1, 2),))
    step_offset = jnp.clip(jax.random.uniform(seeds[13], (INNER,), jnp.float32, -4.0, -2.0), -4.0, -2.0)
    decay_log = jnp.clip(jax.random.uniform(seeds[14], (STATE, INNER), jnp.float32, -11.0, 1.0), -11.0, 1.0)
    direct_skip_weight = jnp.clip(jax.random.uniform(seeds[15], (INNER,), jnp.float32, 0.5, 1.5), 0.5, 1.5)
    mixer_weight = gaussian(seeds[16], (INNER, D), INNER ** -0.5, 0.109375, ((1, 2),))
    attend_gain = jnp.clip(1.0 + 0.1 * jax.random.normal(seeds[17], (D,), jnp.float32), 0.5, 1.5)
    state_gain = jnp.clip(1.0 + 0.1 * jax.random.normal(seeds[18], (D,), jnp.float32), 0.5, 1.5)
    feed_gain = jnp.clip(1.0 + 0.1 * jax.random.normal(seeds[19], (D,), jnp.float32), 0.5, 1.5)
    gate_weight = gaussian(seeds[20], (D, FF), D ** -0.5, 0.15625, ((1, 2),))
    up_weight = gaussian(seeds[21], (D, FF), D ** -0.5, 0.15625, ((1, 2),))
    down_weight = gaussian(seeds[22], (D, FF), FF ** -0.5, 0.078125, ((1, 2),))
    return {"tokens": tokens, "segment_ids": segment_ids, "cotangent": cotangent, "norm_gain": norm_gain, "query_weight": query_weight, "key_weight": key_weight, "value_weight": value_weight, "head_weight": head_weight, "input_weight": input_weight, "filter_weight": filter_weight, "filter_bias": filter_bias, "select_weight": select_weight, "step_weight": step_weight, "step_offset": step_offset, "decay_log": decay_log, "direct_skip_weight": direct_skip_weight, "mixer_weight": mixer_weight, "attend_gain": attend_gain, "state_gain": state_gain, "feed_gain": feed_gain, "gate_weight": gate_weight, "up_weight": up_weight, "down_weight": down_weight}


epsilon = 1e-06
masked = -1e+30
highest = lax.Precision.HIGHEST

@jax.custom_vjp
def low(v):
    return lax.optimization_barrier(v.astype(jnp.bfloat16)).astype(jnp.float32)

@jax.custom_vjp
def low_back(v):
    return v

def low_keep(v):
    return (low(v), None)

def low_pass(kept, grad):
    return (grad,)

def back_keep(v):
    return (v, None)

def back_low(kept, grad):
    return (low(grad),)
low.defvjp(low_keep, low_pass)
low_back.defvjp(back_keep, back_low)

def rounded(value):
    return low_back(low(value))

def matmul(left, right):
    return jnp.dot(left, right, precision=highest, preferred_element_type=jnp.float32)

def inverse_norm(value):
    return lax.rsqrt(lax.optimization_barrier(jnp.mean(value * value, axis=-1, keepdims=True)) + epsilon)

def window_attention(query, keys, values, segment):
    length = query.shape[0]
    groups = HEADS // KEY_HEADS
    grouped = query.reshape(length, KEY_HEADS, groups, HEAD_SIZE)
    keys = keys.reshape(length, KEY_HEADS, HEAD_SIZE)
    values = values.reshape(length, KEY_HEADS, HEAD_SIZE)
    padding = jnp.zeros((WINDOW, KEY_HEADS, HEAD_SIZE), jnp.float32)
    padded_keys = jnp.concatenate([padding, keys], axis=0)
    padded_values = jnp.concatenate([padding, values], axis=0)
    padded_segment = jnp.concatenate([jnp.full((WINDOW,), -1, jnp.int32), segment.astype(jnp.int32)])
    offsets = jnp.arange(QUERY_BLOCK, dtype=jnp.int32)[:, None] + WINDOW - jnp.arange(QUERY_BLOCK + WINDOW, dtype=jnp.int32)[None, :]

    def block(index):
        start = (index * QUERY_BLOCK).astype(jnp.int32)
        rows = lax.dynamic_slice_in_dim(grouped, start, QUERY_BLOCK, 0)
        near_keys = lax.dynamic_slice_in_dim(padded_keys, start, QUERY_BLOCK + WINDOW, 0)
        near_values = lax.dynamic_slice_in_dim(padded_values, start, QUERY_BLOCK + WINDOW, 0)
        near_segment = lax.dynamic_slice_in_dim(padded_segment, start, QUERY_BLOCK + WINDOW, 0)
        row_segment = lax.dynamic_slice_in_dim(segment.astype(jnp.int32), start, QUERY_BLOCK, 0)
        allowed = (offsets >= 0) & (offsets < WINDOW) & (row_segment[:, None] == near_segment[None, :])
        scores = low_back(jnp.einsum('tkgd,mkd->kgtm', rows, near_keys, precision=highest) * 0.125)
        scores = jnp.where(allowed, scores, masked)
        top = lax.optimization_barrier(jnp.max(scores, axis=-1, keepdims=True))
        raised = jnp.exp(scores - top)
        chances = low(raised / lax.optimization_barrier(jnp.sum(raised, axis=-1, keepdims=True)))
        mixed = jnp.einsum('kgtm,mkd->tkgd', chances, near_values, precision=highest)
        return mixed.reshape(QUERY_BLOCK, HEADS * HEAD_SIZE)
    blocks = lax.map(jax.checkpoint(block), jnp.arange(length // QUERY_BLOCK, dtype=jnp.int32))
    return blocks.reshape(length, HEADS * HEAD_SIZE)

def selective_scan(step, scan_input_rows, entry, read, hold, decay):
    length = step.shape[0]

    def stretch(state, pieces):

        def token(carry, item):
            size, value, into, output, keep = item
            factor = jnp.exp(size[None, :] * decay) * keep
            carry = factor * carry + (size * value)[None, :] * into[:, None]
            return (carry, lax.optimization_barrier(jnp.sum(output[:, None] * carry, axis=0)))
        return lax.scan(token, state, pieces)

    def split(value_array):
        return value_array.reshape((length // STRETCH, STRETCH) + value_array.shape[1:])
    begin = jnp.zeros((STATE, INNER), jnp.float32)
    final, outputs = lax.scan(jax.checkpoint(stretch), begin, (split(step), split(scan_input_rows), split(entry), split(read), split(hold)))
    return outputs.reshape(length, INNER)

def sequence_layer(params, tokens, segment):
    norm_gain, query_weight, key_weight, value_weight, head_weight, input_weight, filter_weight, filter_bias, select_weight, step_weight, step_offset, decay_log, direct_skip_weight, mixer_weight, attend_gain, state_gain, feed_gain, gate_weight, up_weight, down_weight = params
    length = tokens.shape[0]
    segment = segment.astype(jnp.int32)
    normed = low(tokens * inverse_norm(tokens) * norm_gain)
    query = rounded(matmul(normed, query_weight))
    keys = rounded(matmul(normed, key_weight))
    values = rounded(matmul(normed, value_weight))
    attended = rounded(window_attention(query, keys, values, segment))
    head_out = low_back(matmul(attended, head_weight))
    entered = matmul(normed, input_weight)
    inner_rows = rounded(entered[:, :INNER])
    gate_input = low_back(entered[:, INNER:])
    padded_rows = jnp.concatenate([jnp.zeros((KERNEL - 1, INNER), jnp.float32), inner_rows], axis=0)
    padded_segment = jnp.concatenate([jnp.full((KERNEL - 1,), -1, jnp.int32), segment])
    filtered = filter_bias + jnp.zeros((length, INNER), jnp.float32)
    for tap in range(KERNEL):
        begin = KERNEL - 1 - tap
        same = (padded_segment[begin:begin + length] == segment).astype(jnp.float32)
        filtered = filtered + filter_weight[tap] * (padded_rows[begin:begin + length] * same[:, None])
    smoothed = low(filtered * jax.nn.sigmoid(filtered))
    projected = low_back(matmul(smoothed, select_weight))
    step_low = low(projected[:, :RANK])
    entry = projected[:, RANK:RANK + STATE]
    read = projected[:, RANK + STATE:]
    unsquashed_step = low_back(matmul(step_low, step_weight.T)) + step_offset
    step = jnp.log1p(jnp.exp(unsquashed_step))
    previous = jnp.concatenate([segment[:1], segment[:-1]])
    hold = (previous == segment).astype(jnp.float32)
    decay = -jnp.exp(decay_log)
    scan_result_rows = selective_scan(step, smoothed, entry, read, hold, decay) + direct_skip_weight * smoothed
    gated = low(scan_result_rows * (gate_input * jax.nn.sigmoid(gate_input)))
    branch = low_back(matmul(gated, mixer_weight))
    hidden = tokens + 0.5 * (head_out * inverse_norm(head_out) * attend_gain + branch * inverse_norm(branch) * state_gain)
    second = low(hidden * inverse_norm(hidden) * feed_gain)
    gate_raw = low_back(matmul(second, gate_weight))
    up_raw = low_back(matmul(second, up_weight))
    activated = low(gate_raw * jax.nn.sigmoid(gate_raw) * up_raw)
    return hidden + low_back(matmul(activated, down_weight.T))

def reference(tokens, segment_ids, cotangent, norm_gain, query_weight, key_weight, value_weight, head_weight, input_weight, filter_weight, filter_bias, select_weight, step_weight, step_offset, decay_log, direct_skip_weight, mixer_weight, attend_gain, state_gain, feed_gain, gate_weight, up_weight, down_weight):
    params = tuple((weight.astype(jnp.float32) for weight in (norm_gain, query_weight, key_weight, value_weight, head_weight, input_weight, filter_weight, filter_bias, select_weight, step_weight, step_offset, decay_log, direct_skip_weight, mixer_weight, attend_gain, state_gain, feed_gain, gate_weight, up_weight, down_weight)))
    inputs = tokens.astype(jnp.float32)

    def forward(inputs, params):

        def one(pair):
            return sequence_layer(params, pair[0], pair[1])
        return lax.map(jax.checkpoint(one), (inputs, segment_ids))
    result, pullback = jax.vjp(forward, inputs, params)
    tokens_gradient, grads = pullback(cotangent.astype(jnp.float32))
    return (result.astype(jnp.bfloat16), tokens_gradient, grads[0], grads[1], grads[2], grads[3], grads[4], grads[5], grads[6], grads[7], grads[8], grads[9], grads[10], grads[11], grads[12], grads[13], grads[14], grads[15], grads[16], grads[17], grads[18], grads[19])
```

```python
import jax
import jax.numpy as jnp
from jax import lax
from jax.experimental import pallas as pl
from jax.experimental.pallas import tpu as pltpu
from jax.sharding import PartitionSpec as P

HEAD_SIZE = 64
WINDOW = 1024


epsilon = 1e-06
masked = -1e30
bf16 = jnp.bfloat16
f32 = jnp.float32
LANES = 128
LOG2E = 1.4426950408889634


def passed_along(block, axis, distance):
    devices = range(lax.axis_size(axis))
    route = [(i - distance, i) for i in devices if i - distance in devices]
    return lax.ppermute(block, axis, route)


def from_ahead(block, distance):
    count = lax.axis_size("wt")
    return lax.ppermute(block, "wt", [((i + distance) % count, i) for i in range(count)])


def picked(blocks, index):
    result = blocks[0]
    for place in range(1, len(blocks)):
        result = jnp.where(index == place, blocks[place], result)
    return result


def gather_tokens(rows, axis=0):
    count = lax.axis_size("wt")
    return jnp.concatenate([rows] + [from_ahead(rows, k) for k in range(1, count)], axis=axis)


def swapped(blocks):
    count = len(blocks)
    return [blocks[0]] + [from_ahead(blocks[count - k], k) for k in range(1, count)]


def in_order(received, axis):
    place = lax.axis_index("wt")
    count = len(received)
    return jnp.concatenate([picked(received, (a - place) % count) for a in range(count)], axis=axis)


def cut_evenly(value, axis):
    return jnp.split(value, lax.axis_size("wt"), axis=axis)


def to_own_tokens(value, tokens=0, columns=1):
    return in_order(swapped(cut_evenly(value, tokens)), columns)


def to_own_columns(value, tokens=0, columns=1):
    count = lax.axis_size("wt")
    place = lax.axis_index("wt")
    owners = cut_evenly(value, columns)
    blocks = [picked(owners, (place + k) % count) for k in range(count)]
    return jnp.concatenate(swapped(blocks), axis=tokens)


def summed_tokens(value, tokens=0):
    blocks = cut_evenly(value, tokens)
    received = swapped([blocks[0]] + [b.astype(bf16) for b in blocks[1:]])
    total = received[0]
    for block in received[1:]:
        total = total + block.astype(f32)
    return total


def own_columns_sum(value):
    count = lax.axis_size("wt")
    place = lax.axis_index("wt")
    owners = cut_evenly(value, 1)
    return sum(swapped([picked(owners, (place + k) % count) for k in range(count)]))


def seq_swap(block, bit):
    count = lax.axis_size("seq")
    return lax.ppermute(block, "seq", [(i, i ^ (1 << bit)) for i in range(count)])


def features_first(value):
    count = lax.axis_size("seq")
    return value.T.reshape(count, value.shape[1] // count, value.shape[0])


def reversed_bits(value, bits):
    return sum(((value >> bit) & 1) << (bits - 1 - bit) for bit in range(bits))


def arrange_kernel(place_ref, left_ref, own_ref, across_ref, beside_ref, taken_ref):
    count, group, _ = left_ref.shape
    bits = count.bit_length() - 1
    for r in range(count):
        taken_ref[r * group : (r + 1) * group, :] = left_ref[place_ref[0] ^ reversed_bits(r, bits)].astype(f32)
    quarter = own_ref.shape[0]
    own_ref[...] = taken_ref[:quarter].astype(bf16)
    across_ref[:quarter] = taken_ref[quarter : 2 * quarter].astype(bf16)
    across_ref[quarter:] = taken_ref[3 * quarter :].astype(bf16)
    beside_ref[...] = taken_ref[2 * quarter : 3 * quarter].astype(bf16)


def shared_features(left):
    count, group, tokens = left.shape
    quarter = count * group // 4
    place = lax.axis_index("seq").astype(jnp.int32).reshape(1)
    whole = lambda rows: pl.BlockSpec((rows, tokens), lambda i, place: (0, 0))
    sizes = [quarter, 2 * quarter, quarter]
    own, across, beside = pl.pallas_call(
        arrange_kernel,
        grid_spec=pltpu.PrefetchScalarGridSpec(
            num_scalar_prefetch=1,
            grid=(1,),
            in_specs=[pl.BlockSpec((count, group, tokens), lambda i, place: (0, 0, 0))],
            out_specs=[whole(size) for size in sizes],
            scratch_shapes=[pltpu.VMEM((count * group, tokens), f32)],
        ),
        out_shape=[jax.ShapeDtypeStruct((size, tokens), bf16) for size in sizes],
        compiler_params=pltpu.CompilerParams(vmem_limit_bytes=24 * 2**20),
        cost_estimate=pl.CostEstimate(flops=0, transcendentals=0, bytes_accessed=8 * quarter * tokens * 2),
        name="arrange",
    )(place, left)
    return own, beside, seq_swap(across, 1)


def quarter_kernel(
    own_ref, beside_ref, across_ref, right_ref, right_across_ref, keep_ref, send_ref, left_in, right_in, total, sent, got
):
    quarter, columns = total.shape
    place = lax.axis_index("seq")
    partner = {"seq": place + 1 - 2 * (place % 2)}
    barrier = pltpu.get_barrier_semaphore()
    pl.semaphore_signal(barrier, inc=1, device_id=partner, device_id_type=pl.DeviceIdType.MESH)
    pl.semaphore_wait(barrier, 1)
    moves = [
        (right_ref, right_in.at[0]),
        (right_across_ref, right_in.at[1]),
        (beside_ref, left_in.at[0]),
        (across_ref.at[pl.ds(quarter, quarter)], left_in.at[1]),
    ]
    copies = [
        pltpu.make_async_remote_copy(
            src_ref=source,
            dst_ref=target,
            send_sem=sent.at[i],
            recv_sem=got.at[i],
            device_id=partner,
            device_id_type=pl.DeviceIdType.MESH,
        )
        for i, (source, target) in enumerate(moves)
    ]
    for copy in copies:
        copy.start()
    chunks = [slice(at, min(at + 512, columns)) for at in range(0, columns, 512)]
    for chunk in chunks:
        total[:, chunk] = jnp.dot(
            own_ref[...], right_ref[:, chunk], preferred_element_type=f32
        ) + jnp.dot(across_ref[:quarter], right_across_ref[:, chunk], preferred_element_type=f32)
    for copy in copies:
        copy.wait()
    half = quarter // 2
    for chunk in chunks:
        result = (
            total[:, chunk]
            + jnp.dot(left_in[0], right_in[0, :, chunk], preferred_element_type=f32)
            + jnp.dot(left_in[1], right_in[1, :, chunk], preferred_element_type=f32)
        )
        keep_ref[:, chunk] = result[:half].astype(bf16)
        send_ref[:, chunk] = result[half:].astype(bf16)


def quarter_gradient(left, right, collective):
    rows, tokens = left[0].shape
    columns = right[0].shape[1]
    vmem = pl.BlockSpec(memory_space=pltpu.VMEM)
    return pl.pallas_call(
        quarter_kernel,
        in_specs=[vmem] * 5,
        out_specs=[vmem] * 2,
        out_shape=[jax.ShapeDtypeStruct((rows // 2, columns), bf16)] * 2,
        scratch_shapes=[
            pltpu.VMEM((2, rows, tokens), bf16),
            pltpu.VMEM((2, tokens, columns), bf16),
            pltpu.VMEM((rows, columns), f32),
            pltpu.SemaphoreType.DMA((4,)),
            pltpu.SemaphoreType.DMA((4,)),
        ],
        compiler_params=pltpu.CompilerParams(
            vmem_limit_bytes=40 * 2**20, collective_id=collective, has_side_effects=True
        ),
        cost_estimate=pl.CostEstimate(flops=0, transcendentals=0, bytes_accessed=1 << 20),
        name="gradient",
    )(*left, *right)


def added(keep, received):
    total = keep.astype(f32) + received.astype(f32)
    half = total.shape[0] // 2
    return total[:half].astype(bf16), total[half:].astype(bf16)


class Gradient:
    def __init__(self, left, right, collective):
        self.left, self.right, self.collective = left, (right, seq_swap(right, 1)), collective
        self.bits = lax.axis_size("seq").bit_length() - 1
        self.bit = 2
        self.total = None

    def start(self):
        self.received = seq_swap(self.send, self.bit)
        self.bit += 1

    def finish(self):
        if self.bit == 2:
            self.keep, self.send = quarter_gradient(self.left, self.right, self.collective)
        elif self.bit < self.bits:
            self.keep, self.send = added(self.keep, self.received)
        else:
            self.total = self.keep.astype(f32) + self.received.astype(f32)

    def state(self):
        return (self.keep, self.send) if self.total is None else self.total

    def set_state(self, state):
        if self.total is None:
            self.keep, self.send = state
        else:
            self.total = state


def advance(chain, gradients):
    for gradient in gradients:
        gradient.finish()
    chain, states = lax.optimization_barrier((chain, [g.state() for g in gradients]))
    for gradient, state in zip(gradients, states):
        gradient.set_state(state)
        if gradient.total is None:
            gradient.start()
    return chain


def completed_all(gradients):
    while any(gradient.total is None for gradient in gradients):
        for gradient in gradients:
            gradient.finish()
            if gradient.total is None:
                gradient.start()
    return [gradient.total for gradient in gradients]


def column_chunks(value, chunks):
    width = value.shape[1] // lax.axis_size("wt")
    piece = -(-width // chunks // LANES) * LANES
    owners = cut_evenly(value, 1)
    return [
        to_own_columns(jnp.concatenate([owner[:, at : at + piece] for owner in owners], axis=1))
        for at in range(0, width, piece)
    ]


def completed(gradient):
    while gradient.total is None:
        gradient.finish()
        if gradient.total is None:
            gradient.start()
    return gradient.total


def lane_blocks(inner):
    blocks = inner // LANES
    return next(n for n in (5, 4, 3, 2, 1) if blocks % n == 0)

def cut_lanes(value):
    return [value[:, i * LANES : (i + 1) * LANES] for i in range(value.shape[1] // LANES)]

def spread(ref, tile, row, states):
    values = ref[tile, row : row + 1, :]
    return [jnp.broadcast_to(part, (states, LANES)) for part in cut_lanes(values)]


def advanced(size_ref, inject_ref, entry_ref, decay, tile, row, state):
    states = entry_ref.shape[1]
    into = entry_ref[tile * 8 + row]
    return tuple(
        jnp.exp2(size * rate) * old + inject * into
        for size, inject, rate, old in zip(
            spread(size_ref, tile, row, states), spread(inject_ref, tile, row, states), decay, state
        )
    )


def no_state(decay_ref):
    return tuple(jnp.zeros_like(part) for part in cut_lanes(decay_ref[...]))


def state_kernel(size_ref, inject_ref, entry_ref, decay_ref, last_ref):
    decay = cut_lanes(decay_ref[...])

    def tokens(tile, state):
        for row in range(8):
            state = advanced(size_ref, inject_ref, entry_ref, decay, tile, row, state)
        return state

    state = lax.fori_loop(0, size_ref.shape[0], tokens, no_state(decay_ref))
    last_ref[...] = jnp.concatenate(state, axis=1)


def output_kernel(size_ref, inject_ref, entry_ref, read_ref, decay_ref, begin_ref, out_ref):
    decay = cut_lanes(decay_ref[...])

    def tokens(tile, state):
        for row in range(8):
            state = advanced(size_ref, inject_ref, entry_ref, decay, tile, row, state)
            output = read_ref[tile * 8 + row]
            for i, part in enumerate(state):
                out_ref[tile, row : row + 1, i * LANES : (i + 1) * LANES] = jnp.sum(
                    output * part, axis=0, keepdims=True
                )
        return state

    lax.fori_loop(0, size_ref.shape[0], tokens, tuple(cut_lanes(begin_ref[...])))


def adjoint_kernel(size_ref, back_ref, read_ref, decay_ref, first_ref):
    states = decay_ref.shape[0]
    decay = cut_lanes(decay_ref[...])
    tiles = size_ref.shape[0]

    def tokens(turn, carry):
        tile = tiles - 1 - turn
        for row in reversed(range(8)):
            output = read_ref[tile * 8 + row]
            carry = tuple(
                jnp.exp2(size * rate) * (output * back + old)
                for size, back, rate, old in zip(
                    spread(size_ref, tile, row, states), spread(back_ref, tile, row, states), decay, carry
                )
            )
        return carry

    carry = lax.fori_loop(0, tiles, tokens, no_state(decay_ref))
    first_ref[...] = jnp.concatenate(carry, axis=1)


def gradient_kernel(
    size_ref,
    inject_ref,
    back_ref,
    entry_ref,
    read_ref,
    decay_ref,
    rate_ref,
    begin_ref,
    end_ref,
    through_ref,
    sized_ref,
    entry_back_ref,
    read_back_ref,
    decay_back_ref,
    prior_ref,
):
    states = decay_ref.shape[0]
    decay = cut_lanes(decay_ref[...])
    tiles = size_ref.shape[0]

    @pl.when(pl.program_id(0) == 0)
    def _():
        entry_back_ref[...] = jnp.zeros_like(entry_back_ref)
        read_back_ref[...] = jnp.zeros_like(read_back_ref)

    def forward(tile, state):
        for row in range(8):
            for i, part in enumerate(state):
                prior_ref[tile * 8 + row, :, i * LANES : (i + 1) * LANES] = part
            state = advanced(size_ref, inject_ref, entry_ref, decay, tile, row, state)
        return state

    last = lax.fori_loop(0, tiles, forward, tuple(cut_lanes(begin_ref[...])))

    def backward(turn, carry):
        tile = tiles - 1 - turn
        arriving, current, total = carry
        for row in reversed(range(8)):
            t = tile * 8 + row
            into = entry_ref[t]
            output = read_ref[t]
            sizes = spread(size_ref, tile, row, states)
            injects = spread(inject_ref, tile, row, states)
            backs = spread(back_ref, tile, row, states)
            entry_back = entry_back_ref[t]
            read_back = read_back_ref[t]
            new_arriving, new_current, new_total = [], [], []
            for k in range(len(decay)):
                lanes = slice(k * LANES, (k + 1) * LANES)
                prior = prior_ref[t, :, lanes]
                adjoint = output * backs[k] + arriving[k]
                leaving = jnp.exp2(sizes[k] * decay[k]) * adjoint
                weighted = leaving * prior
                through_ref[tile, row : row + 1, lanes] = jnp.sum(adjoint * into, axis=0, keepdims=True)
                sized_ref[tile, row : row + 1, lanes] = jnp.sum(
                    weighted * rate_ref[:, lanes], axis=0, keepdims=True
                )
                entry_back = entry_back + adjoint * injects[k]
                read_back = read_back + current[k] * backs[k]
                new_total.append(total[k] + weighted * sizes[k])
                new_arriving.append(leaving)
                new_current.append(prior)
            entry_back_ref[t] = entry_back
            read_back_ref[t] = read_back
            arriving, current, total = new_arriving, new_current, new_total
        return tuple(arriving), tuple(current), tuple(total)

    arriving = tuple(cut_lanes(end_ref[...]))
    _, _, total = lax.fori_loop(0, tiles, backward, (arriving, last, no_state(decay_ref)))
    decay_back_ref[...] = jnp.concatenate(total, axis=1)


def scan_call(body, name, token_args, wide_args, state_args, outs, scratch=False, flops=0):
    rows, inner = token_args[0].shape
    states = state_args[0].shape[0]
    width = lane_blocks(inner) * LANES
    token = pl.BlockSpec((rows // 8, 8, width), lambda i: (0, 0, i))
    wide = pl.BlockSpec((rows, states, LANES), lambda i: (0, 0, 0))
    state = pl.BlockSpec((states, width), lambda i: (0, i))
    kinds = {
        "token": (token, jax.ShapeDtypeStruct((rows // 8, 8, inner), f32)),
        "wide": (wide, jax.ShapeDtypeStruct((rows, states, LANES), f32)),
        "state": (state, jax.ShapeDtypeStruct((states, inner), f32)),
    }
    size = rows * states * inner
    results = pl.pallas_call(
        body,
        grid=(inner // width,),
        in_specs=[token] * len(token_args) + [wide] * len(wide_args) + [state] * len(state_args),
        out_specs=[kinds[k][0] for k in outs],
        out_shape=[kinds[k][1] for k in outs],
        scratch_shapes=[pltpu.VMEM((rows, states, width), f32)] if scratch else [],
        compiler_params=pltpu.CompilerParams(vmem_limit_bytes=40 * 2**20),
        cost_estimate=pl.CostEstimate(flops=0, transcendentals=0, bytes_accessed=flops << 18),
        name=name,
    )(*[arg.reshape(rows // 8, 8, inner) for arg in token_args], *wide_args, *state_args)
    return [r.reshape(rows, inner) if k == "token" else r for k, r in zip(outs, results)]


def entering(total, part, rate, reverse):
    count = lax.axis_size("seq")
    sign = -1 if reverse else 1
    packed = jnp.concatenate([total[None], part], axis=0)
    near = passed_along(packed, "seq", sign)
    far = passed_along(packed, "seq", 2 * sign)
    total, part = near[0] + far[0], jnp.exp2(near[0] * rate) * far[1:] + near[1:]
    distance = 2
    while distance < count:
        received = passed_along(jnp.concatenate([total[None], part], axis=0), "seq", distance * sign)
        part = jnp.exp2(total * rate) * received[1:] + part
        total = total + received[0]
        distance *= 2
    return part


def summed_everywhere(parts):
    sizes = [part.size for part in parts]
    packed = jnp.concatenate([part.reshape(-1) for part in parts])
    packed = jnp.pad(packed, (0, -packed.size % 1024)).reshape(-1, 128)
    for axis in ("seq", "wt"):
        count = lax.axis_size(axis)
        bit = 1
        while bit < count:
            packed = packed + lax.ppermute(packed, axis, [(i, i ^ bit) for i in range(count)])
            bit *= 2
    packed = packed.reshape(-1)
    result, begin = [], 0
    for part, size in zip(parts, sizes):
        result.append(packed[begin : begin + size].reshape(part.shape))
        begin += size
    return result


def product(left, right):
    return jnp.dot(left, right, preferred_element_type=jnp.float32)


def left_product(left, right):
    return lax.dot_general(
        left, right, (((0,), (0,)), ((), ())), preferred_element_type=jnp.float32
    )


def right_product(left, right):
    return lax.dot_general(
        left, right, (((1,), (1,)), ((), ())), preferred_element_type=jnp.float32
    )


def transposed_dot(left, right):
    return lax.dot_general(left, right, (((0,), (0,)), ((), ())), preferred_element_type=f32)


def heads_beside(value):
    heads = value.shape[0] // HEAD_SIZE
    return jnp.concatenate(
        [value[h * HEAD_SIZE : (h + 1) * HEAD_SIZE] for h in range(heads)], axis=1
    )


def store_heads(ref, value):
    rows = ref.shape[1]
    for h in range(ref.shape[0] // HEAD_SIZE):
        ref[h * HEAD_SIZE : (h + 1) * HEAD_SIZE, :] = value[:, h * rows : (h + 1) * rows].astype(ref.dtype)


def chance_table(query, keys, bias):
    heads = query.shape[1] // bias.shape[1]
    scores = transposed_dot(keys, query) + jnp.concatenate([bias] * heads, axis=1)
    raised = jnp.exp(scores - jnp.max(scores, axis=0, keepdims=True))
    return raised * (1.0 / jnp.sum(raised, axis=0, keepdims=True))


def attend_kernel(query_ref, keys_ref, values_ref, bias_ref, out_ref):
    query = heads_beside(query_ref[...]) * bf16(0.125)
    chances = chance_table(query, keys_ref[...], bias_ref[...]).astype(bf16)
    store_heads(out_ref, jnp.dot(values_ref[...], chances, preferred_element_type=f32))


def attend_back_kernel(query_ref, keys_ref, values_ref, back_ref, bias_ref, query_back_ref, keys_back_ref, values_back_ref):
    query = heads_beside(query_ref[...]) * bf16(0.125)
    back = heads_beside(back_ref[...])
    weights = chance_table(query, keys_ref[...], bias_ref[...])
    values_back_ref[...] = right_product(back, weights.astype(bf16))
    delta = transposed_dot(values_ref[...], back)
    weighted = weights * delta
    scores_back = (weighted - weights * jnp.sum(weighted, axis=0, keepdims=True)).astype(bf16)
    store_heads(query_back_ref, jnp.dot(keys_ref[...], scores_back, preferred_element_type=f32) * 0.125)
    keys_back_ref[...] = right_product(query, scores_back)


def attention_call(body, name, wide, near, bias, outs, flops):
    span, rows = bias.shape
    key_heads = near[0].shape[0] // HEAD_SIZE
    width = wide[0].shape[0] // key_heads
    wide_spec = pl.BlockSpec((width, rows), lambda k: (k, 0))
    near_spec = pl.BlockSpec((HEAD_SIZE, span), lambda k: (k, 0))
    kinds = {
        "wide": (wide_spec, jax.ShapeDtypeStruct(wide[0].shape, bf16)),
        "near": (near_spec, jax.ShapeDtypeStruct(near[0].shape, f32)),
    }
    size = key_heads * span * rows * (width // HEAD_SIZE)
    return pl.pallas_call(
        body,
        grid=(key_heads,),
        in_specs=[wide_spec] + [near_spec] * 2 + [wide_spec] * (len(wide) - 1)
        + [pl.BlockSpec((span, rows), lambda k: (0, 0))],
        out_specs=[kinds[k][0] for k in outs],
        out_shape=[kinds[k][1] for k in outs],
        compiler_params=pltpu.CompilerParams(vmem_limit_bytes=56 * 2**20),
        cost_estimate=pl.CostEstimate(flops=0, transcendentals=0, bytes_accessed=flops << 19),
        name=name,
    )(wide[0], *near, *wide[1:], bias)


def outer_product(left, right):
    return lax.dot_general(left, right, (((0,), (1,)), ((), ())), preferred_element_type=f32)


def inverse_norm(value):
    return lax.rsqrt(jnp.mean(value * value, axis=-1, keepdims=True) + epsilon)


def norm_back(value, scale, incoming):
    return scale * incoming - scale * scale * scale * value * jnp.mean(
        incoming * value, axis=-1, keepdims=True
    )


def silu_slope(value):
    sigma = jax.nn.sigmoid(value)
    return sigma * (1.0 + value * (1.0 - sigma))


def gather_columns(own):
    count = lax.axis_size("wt")
    turned = own.T
    return in_order([turned] + [from_ahead(turned, k) for k in range(1, count)], 0)


def feed_block(second_rows, back_rows, gate_cols, up_cols, down_cols):
    gate_raw = product(second_rows, gate_cols)
    up_raw = product(second_rows, up_cols)
    sigma_gate = jax.nn.sigmoid(gate_raw)
    activated = (gate_raw * sigma_gate * up_raw).astype(jnp.bfloat16)
    feed_out = right_product(activated, down_cols)
    delta_act = product(back_rows, down_cols)
    delta_gate = (delta_act * up_raw * silu_slope(gate_raw)).astype(jnp.bfloat16)
    delta_up = (delta_act * gate_raw * sigma_gate).astype(jnp.bfloat16)
    delta_second = right_product(delta_gate, gate_cols) + right_product(delta_up, up_cols)
    return (feed_out, delta_second, activated, delta_gate, delta_up)


def per_device(
    tokens,
    segment_ids,
    cotangent,
    norm_gain,
    query_weight,
    key_weight,
    value_weight,
    head_weight,
    input_weight,
    filter_weight,
    filter_bias,
    select_weight,
    step_weight,
    step_offset,
    decay_log,
    direct_skip_weight,
    mixer_weight,
    attend_gain,
    state_gain,
    feed_gain,
    gate_weight,
    up_weight,
    down_weight,
):
    rows = tokens.shape[1]
    model = tokens.shape[2]
    inner = filter_weight.shape[1]
    kernel = filter_weight.shape[0]
    states = decay_log.shape[0]
    start = lax.axis_index("seq") * rows
    whole_segment = segment_ids[0]
    padded_segment = jnp.concatenate([jnp.full((WINDOW,), -1, jnp.int32), whole_segment])
    segment = lax.dynamic_slice_in_dim(whole_segment, start, rows)
    inputs = tokens[0].astype(jnp.float32)
    upstream = cotangent[0].astype(jnp.float32)
    both_tokens = gather_tokens(tokens[0])
    select_full = gather_columns(select_weight)
    step_full = gather_columns(step_weight)
    both_back = gather_tokens(cotangent[0])
    rank = step_full.shape[0]
    first_scale = inverse_norm(inputs)
    both_inputs = both_tokens.astype(jnp.float32)
    both_normed = (both_inputs * inverse_norm(both_inputs) * norm_gain).astype(jnp.bfloat16)
    normed_shared = shared_features(features_first(both_normed))
    back_shared = shared_features(features_first(both_back))
    pairs = jnp.stack(
        [outer_product(weight, both_normed).astype(bf16) for weight in (key_weight, value_weight)]
    )
    pairs = to_own_tokens(pairs, 2, 1)
    entered = to_own_tokens(product(both_normed, input_weight).astype(jnp.bfloat16))
    query = to_own_tokens(outer_product(query_weight, both_normed).astype(jnp.bfloat16), 1, 0)
    hops = -(-WINDOW // (4 * rows))
    near = jnp.concatenate(
        [pairs] + [passed_along(pairs, "seq", 4 * hop) for hop in range(1, hops + 1)], axis=2
    )
    for bit in (1, 0):
        near = jnp.concatenate([near, seq_swap(near, bit)], axis=2)
    seq_place = lax.axis_index("seq")
    block_places = jnp.stack(
        [(seq_place ^ other) - 4 * hop for other in (0, 2, 1, 3) for hop in range(hops + 1)]
    )
    near_place = (block_places[:, None] * rows + jnp.arange(rows, dtype=jnp.int32)[None, :]).reshape(-1)
    near_segment = jnp.where(
        block_places[:, None] >= 0,
        jnp.take(whole_segment.reshape(-1, rows), jnp.maximum(block_places, 0), axis=0),
        -1,
    ).reshape(-1)
    distance = start + jnp.arange(rows, dtype=jnp.int32)[None, :] - near_place[:, None]
    allowed = (distance >= 0) & (distance < WINDOW) & (segment[None, :] == near_segment[:, None])
    bias = jnp.where(allowed, 0.0, masked)
    (attended,) = attention_call(attend_kernel, "attend", [query], [near[0], near[1]], bias, ["wide"], 2)
    both_attended = gather_tokens(attended, 1)
    attended_shared = shared_features(
        both_attended.reshape(lax.axis_size("seq"), -1, both_attended.shape[1])
    )
    head_out = to_own_tokens(left_product(both_attended, head_weight).astype(bf16)).astype(f32)
    inner_rows = entered[:, :inner]
    gate_input = entered[:, inner:].astype(jnp.float32)
    before = passed_along(inner_rows[rows - kernel + 1 :], "seq", 1)
    extended = jnp.concatenate([before, inner_rows], axis=0).astype(jnp.float32)
    edge_segment = lax.dynamic_slice_in_dim(
        padded_segment, start + WINDOW - kernel + 1, rows + kernel - 1
    )
    taps = []
    sames = []
    filtered = filter_bias + jnp.zeros((rows, inner), jnp.float32)
    for tap in range(kernel):
        begin = kernel - 1 - tap
        same = (edge_segment[begin : begin + rows] == segment).astype(jnp.float32)
        kept_rows = extended[begin : begin + rows] * same[:, None]
        taps.append(kept_rows)
        sames.append(same)
        filtered = filtered + filter_weight[tap] * kept_rows
    smoothed = (filtered * jax.nn.sigmoid(filtered)).astype(jnp.bfloat16)
    scan_input_rows = smoothed.astype(jnp.float32)
    smoothed_shared = shared_features(features_first(smoothed))
    projected = right_product(smoothed, select_full)
    step_low = projected[:, :rank].astype(jnp.bfloat16)
    entry = projected[:, rank : rank + states]
    read = projected[:, rank + states :]
    unsquashed_step = product(step_low, step_full) + step_offset
    step = jnp.log1p(jnp.exp(unsquashed_step))
    previous = lax.dynamic_slice_in_dim(padded_segment, start + WINDOW - 1, rows)
    hold = (previous == segment).astype(jnp.float32)
    decay = -jnp.exp(decay_log)
    rate = decay * LOG2E
    size = jnp.where(hold[:, None] == 0.0, 1e30, step)
    inject = step * scan_input_rows
    entry_wide = jnp.broadcast_to(entry[:, :, None], (rows, states, LANES))
    read_wide = jnp.broadcast_to(read[:, :, None], (rows, states, LANES))
    total = jnp.sum(size, axis=0)
    (last,) = scan_call(state_kernel, "scan_state", [size, inject], [entry_wide], [rate], ["state"], flops=4)
    begin_state = entering(total, last, rate, False)
    (scanned,) = scan_call(
        output_kernel, "scan_output", [size, inject], [entry_wide, read_wide], [rate, begin_state], ["token"], flops=6
    )
    scan_result_rows = scanned + direct_skip_weight * scan_input_rows
    sigma_input = jax.nn.sigmoid(gate_input)
    silu_input = gate_input * sigma_input
    gated = (scan_result_rows * silu_input).astype(jnp.bfloat16)
    both_gated = gather_tokens(gated)
    gated_shared = shared_features(features_first(both_gated))
    branch = to_own_tokens(product(both_gated, mixer_weight).astype(jnp.bfloat16)).astype(f32)
    head_scale = inverse_norm(head_out)
    branch_scale = inverse_norm(branch)
    hidden = inputs + 0.5 * (
        head_out * head_scale * attend_gain + branch * branch_scale * state_gain
    )
    second_scale = inverse_norm(hidden)
    second = (hidden * second_scale * feed_gain).astype(jnp.bfloat16)
    both_second = gather_tokens(second)
    feed_part, second_part, activated, feed_gate, feed_up = feed_block(
        both_second, both_back, gate_weight, up_weight, down_weight
    )
    second_shared = shared_features(features_first(both_second))
    down = Gradient(back_shared, activated, 1)
    gate = Gradient(second_shared, feed_gate, 1)
    up = Gradient(second_shared, feed_up, 1)
    delta_second = summed_tokens(second_part)
    feed_out = summed_tokens(feed_part)
    result = (hidden + feed_out).astype(jnp.bfloat16)
    feed_sum = jnp.sum(delta_second * hidden * second_scale, axis=0)
    delta_hidden = upstream + norm_back(hidden, second_scale, delta_second * feed_gain)
    half = 0.5 * delta_hidden
    attend_sum = jnp.sum(half * head_out * head_scale, axis=0)
    state_sum = jnp.sum(half * branch * branch_scale, axis=0)
    delta_head = norm_back(head_out, head_scale, half * attend_gain).astype(jnp.bfloat16)
    delta_branch = norm_back(branch, branch_scale, half * state_gain).astype(jnp.bfloat16)
    delta_head, delta_branch = advance((delta_head, delta_branch), [down])
    both_delta_head = to_own_columns(delta_head)
    both_delta_branch = to_own_columns(delta_branch)
    head = Gradient(attended_shared, both_delta_head, 2)
    mixer = Gradient(gated_shared, both_delta_branch, 3)
    delta_gated = summed_tokens(right_product(both_delta_branch, mixer_weight))
    delta_attended = summed_tokens(right_product(head_weight, both_delta_head), 1).astype(bf16)
    delta_query, key_near, value_near = attention_call(
        attend_back_kernel, "attend_back", [query, delta_attended], [near[0], near[1]], bias, ["wide", "near", "near"], 5
    )
    delta_near = jnp.stack([key_near, value_near])
    for bit in (0, 1):
        half = delta_near.shape[2] // 2
        received = seq_swap(delta_near[:, :, half:].astype(bf16), bit)
        delta_near = delta_near[:, :, :half] + received.astype(f32)
    delta_pairs = delta_near[:, :, :rows]
    for hop in range(1, hops + 1):
        piece = delta_near[:, :, hop * rows : (hop + 1) * rows].astype(bf16)
        delta_pairs = delta_pairs + passed_along(piece, "seq", -4 * hop).astype(f32)
    delta_pairs = delta_pairs.astype(jnp.bfloat16)
    both_qkv = jnp.concatenate(
        [
            to_own_columns(delta_query, 1, 0),
            to_own_columns(delta_pairs[0], 1, 0),
            to_own_columns(delta_pairs[1], 1, 0),
        ],
        axis=0,
    ).T
    qkv_sums = Gradient(normed_shared, both_qkv, 4)
    delta_scan_output = delta_gated * silu_input
    delta_gate = (delta_gated * scan_result_rows * silu_slope(gate_input)).astype(jnp.bfloat16)
    skip_sum = jnp.sum(delta_scan_output * scan_input_rows, axis=0)
    (first,) = scan_call(adjoint_kernel, "scan_adjoint", [size, delta_scan_output], [read_wide], [rate], ["state"], flops=4)
    end_state = entering(total, first, rate, True)
    end_state = advance(end_state, [down, gate, up, head, mixer])
    through, sized, entry_back, read_back, decay_acc = scan_call(
        gradient_kernel,
        "scan_gradient",
        [size, inject, delta_scan_output],
        [entry_wide, read_wide],
        [rate, decay, begin_state, end_state],
        ["token", "token", "wide", "wide", "state"],
        scratch=True,
        flops=20,
    )
    through, sized, decay_acc = advance((through, sized, decay_acc), [down, gate, up, head, mixer])
    decay_sum = decay_acc * decay
    delta_scan_input = delta_scan_output * direct_skip_weight + through * step
    delta_unsquashed_step = (sized + through * scan_input_rows) * jax.nn.sigmoid(unsquashed_step)
    offset_sum = jnp.sum(delta_unsquashed_step, axis=0)
    raw_low = delta_unsquashed_step.astype(jnp.bfloat16)
    delta_lowrank_step = right_product(raw_low, step_full)
    delta_projected = jnp.concatenate(
        [
            delta_lowrank_step,
            jnp.sum(entry_back, axis=-1),
            jnp.sum(read_back, axis=-1),
        ],
        axis=1,
    ).astype(jnp.bfloat16)
    delta_scan_input = delta_scan_input + product(delta_projected, select_full)
    delta_filtered = delta_scan_input * silu_slope(filtered)
    bias_sum = jnp.sum(delta_filtered, axis=0)
    filter_sums = jnp.stack([jnp.sum(delta_filtered * kept_rows, axis=0) for kept_rows in taps])
    shares = [delta_filtered * filter_weight[tap] * sames[tap][:, None] for tap in range(kernel)]
    leaving = jnp.stack(
        [
            sum(shares[tap][tap - back] for tap in range(back, kernel))
            for back in range(kernel - 1, 0, -1)
        ]
    )
    arrived = passed_along(leaving.astype(jnp.bfloat16), "seq", -1).astype(jnp.float32)
    delta_inner = sum(jnp.pad(share[tap:], ((0, tap), (0, 0))) for tap, share in enumerate(shares))
    delta_inner = delta_inner + jnp.pad(arrived, ((rows - kernel + 1, 0), (0, 0)))
    delta_entered = jnp.concatenate([delta_inner.astype(jnp.bfloat16), delta_gate], axis=1)
    delta_entered = advance(delta_entered, [up, head, mixer])
    both_entered = column_chunks(delta_entered, 4)
    widths = (query_weight.shape[1], key_weight.shape[1], value_weight.shape[1])
    cuts = (0, widths[0], widths[0] + widths[1], sum(widths))
    delta_normed = right_product(jnp.concatenate(both_entered, axis=1), input_weight)
    for place, weight in enumerate((query_weight, key_weight, value_weight)):
        delta_normed = delta_normed + right_product(both_qkv[:, cuts[place] : cuts[place + 1]], weight)
    delta_normed = summed_tokens(delta_normed)
    norm_sum = jnp.sum(delta_normed * inputs * first_scale, axis=0)
    delta_tokens = delta_hidden + norm_back(inputs, first_scale, delta_normed * norm_gain)
    select_sums = Gradient(smoothed_shared, delta_projected, 5)
    step_sums = Gradient(shared_features(features_first(raw_low)), step_low, 6)
    input_sums = [
        Gradient(normed_shared, part, 7 if part.shape == both_entered[0].shape else 8) for part in both_entered
    ]
    qkv_gradient = completed(qkv_sums)
    query_gradient, key_gradient, value_gradient = (
        qkv_gradient[:, cuts[place] : cuts[place + 1]] for place in range(3)
    )
    select_gradient = own_columns_sum(completed(select_sums))
    step_gradient = own_columns_sum(completed(step_sums))
    input_gradient = jnp.concatenate(completed_all(input_sums), axis=1)
    down_gradient, gate_gradient, up_gradient, head_gradient, mixer_gradient = (
        completed(gradient) for gradient in (down, gate, up, head, mixer)
    )
    feed_total, attend_total, state_total, skip_total, decay_total, offset_total = lax.psum(
        (feed_sum, attend_sum, state_sum, skip_sum, decay_sum, offset_sum), ("seq", "wt")
    )
    norm_total, filter_total, bias_total = summed_everywhere((norm_sum, filter_sums, bias_sum))
    return (
        result[None],
        delta_tokens[None],
        norm_total,
        query_gradient,
        key_gradient,
        value_gradient,
        head_gradient,
        input_gradient,
        filter_total,
        bias_total,
        select_gradient,
        step_gradient,
        offset_total,
        decay_total,
        skip_total,
        mixer_gradient,
        attend_total,
        state_total,
        feed_total,
        gate_gradient,
        up_gradient,
        down_gradient,
    )


def solution(mesh):
    placed = (
        P("wt", "seq", None),
        P("wt", None),
        P("wt", "seq", None),
        P(),
        P(None, "wt"),
        P(None, "wt"),
        P(None, "wt"),
        P(None, "wt"),
        P(None, "wt"),
        P(),
        P(),
        P(None, "wt"),
        P(None, "wt"),
        P(),
        P(),
        P(),
        P(None, "wt"),
        P(),
        P(),
        P(),
        P(None, "wt"),
        P(None, "wt"),
        P(None, "wt"),
    )
    return jax.shard_map(
        per_device,
        mesh=mesh,
        in_specs=placed,
        out_specs=(
            P("wt", "seq", None),
            P("wt", "seq", None),
            P(),
            P("seq", "wt"),
            P("seq", "wt"),
            P("seq", "wt"),
            P("seq", "wt"),
            P("seq", "wt"),
            P(),
            P(),
            P("seq", "wt"),
            P("seq", "wt"),
            P(),
            P(),
            P(),
            P("seq", "wt"),
            P(),
            P(),
            P(),
            P("seq", "wt"),
            P("seq", "wt"),
            P("seq", "wt"),
        ),
        check_vma=False,
    )
```

```python
import functools

import jax
import jax.numpy as jnp
from jax import lax
from jax.experimental import pallas as pl
from jax.experimental.pallas import tpu as pltpu
from jax.sharding import PartitionSpec as P

HEAD_SIZE = 64
WINDOW = 1024


epsilon = 1e-06
masked = -1e30
bf16 = jnp.bfloat16
f32 = jnp.float32
LANES = 128
LOG2E = 1.4426950408889634


def passed_along(block, axis, distance):
    devices = range(lax.axis_size(axis))
    route = [(i - distance, i) for i in devices if i - distance in devices]
    return lax.ppermute(block, axis, route)


def from_ahead(block, distance):
    count = lax.axis_size("wt")
    return lax.ppermute(block, "wt", [((i + distance) % count, i) for i in range(count)])


def picked(blocks, index):
    result = blocks[0]
    for place in range(1, len(blocks)):
        result = jnp.where(index == place, blocks[place], result)
    return result


def gather_tokens(rows, axis=0):
    count = lax.axis_size("wt")
    return jnp.concatenate([rows] + [from_ahead(rows, k) for k in range(1, count)], axis=axis)


def swapped(blocks):
    count = len(blocks)
    return [blocks[0]] + [from_ahead(blocks[count - k], k) for k in range(1, count)]


def in_order(received, axis):
    place = lax.axis_index("wt")
    count = len(received)
    return jnp.concatenate([picked(received, (a - place) % count) for a in range(count)], axis=axis)


def cut_evenly(value, axis):
    return jnp.split(value, lax.axis_size("wt"), axis=axis)


def to_own_tokens(value, tokens=0, columns=1):
    return in_order(swapped(cut_evenly(value, tokens)), columns)


def to_own_columns(value, tokens=0, columns=1):
    count = lax.axis_size("wt")
    place = lax.axis_index("wt")
    owners = cut_evenly(value, columns)
    blocks = [picked(owners, (place + k) % count) for k in range(count)]
    return jnp.concatenate(swapped(blocks), axis=tokens)


def summed_tokens(value, tokens=0):
    blocks = cut_evenly(value, tokens)
    received = swapped([blocks[0]] + [b.astype(bf16) for b in blocks[1:]])
    total = received[0]
    for block in received[1:]:
        total = total + block.astype(f32)
    return total


def own_columns_sums(values):
    count = lax.axis_size("wt")
    place = lax.axis_index("wt")
    widths = [value.shape[1] // count for value in values]
    owners = [jnp.concatenate(parts, axis=1) for parts in zip(*(cut_evenly(value, 1) for value in values))]
    total = sum(swapped([picked(owners, (place + k) % count) for k in range(count)]))
    return [total[:, sum(widths[:i]) : sum(widths[: i + 1])] for i in range(len(widths))]


def taking(microseconds):
    return pl.CostEstimate(flops=0, transcendentals=0, bytes_accessed=microseconds * 30_000)


def seq_swap(block, bit):
    count = lax.axis_size("seq")
    return lax.ppermute(block, "seq", [(i, i ^ (1 << bit)) for i in range(count)])


def reversed_bits(value, bits):
    return sum(((value >> bit) & 1) << (bits - 1 - bit) for bit in range(bits))


def arrange_kernel(turned, pieces, place_ref, left_ref, own_ref, across_ref, beside_ref, groups_ref, taken_ref):
    count, _, _ = groups_ref.shape
    bits = count.bit_length() - 1
    left = left_ref[...].astype(f32)
    left = left.T if turned else left
    group = left.shape[0] // count
    for r in range(count):
        groups_ref[r, :group, :] = left[r * group : (r + 1) * group]
    quarter, unit = own_ref.shape[0], group // pieces
    for r in range(count):
        for piece in range(pieces):
            begin = r // (count // 4) * quarter + piece * (quarter // pieces) + r % (count // 4) * unit
            taken_ref[begin : begin + unit, :] = groups_ref[
                place_ref[0] ^ reversed_bits(r, bits), piece * unit : (piece + 1) * unit, :
            ]
    own_ref[...] = taken_ref[:quarter].astype(bf16)
    across_ref[:quarter] = taken_ref[quarter : 2 * quarter].astype(bf16)
    across_ref[quarter:] = taken_ref[3 * quarter :].astype(bf16)
    beside_ref[...] = taken_ref[2 * quarter : 3 * quarter].astype(bf16)


def shared_features(left, model, turned=True, order=()):
    count = lax.axis_size("seq")
    tokens, features = left.shape if turned else left.shape[::-1]
    quarter = features // 4
    place = lax.axis_index("seq").astype(jnp.int32).reshape(1)
    whole = lambda shape: pl.BlockSpec(shape, lambda i, place: (0, 0))
    shapes = [(quarter, tokens), (2 * quarter, tokens), (quarter, tokens)]
    own, across, beside = pl.pallas_call(
        ignoring(functools.partial(arrange_kernel, turned, features // model), 2, len(order)),
        grid_spec=pltpu.PrefetchScalarGridSpec(
            num_scalar_prefetch=1,
            grid=(1,),
            in_specs=[whole(left.shape)] + [pl.BlockSpec(memory_space=pl.ANY)] * len(order),
            out_specs=[whole(shape) for shape in shapes],
            scratch_shapes=[
                pltpu.VMEM((count, -(-features // count // 8) * 8, tokens), f32),
                pltpu.VMEM((features, tokens), f32),
            ],
        ),
        out_shape=[jax.ShapeDtypeStruct(shape, bf16) for shape in shapes],
        compiler_params=pltpu.CompilerParams(vmem_limit_bytes=32 * 2**20),
        cost_estimate=taking(2),
        name="arrange",
    )(place, left, *order)
    return own, beside, seq_swap(across, 1)


def quarter_kernel(parts, counts, *refs):
    lefts = [refs[3 * i : 3 * i + 3] for i in range(counts[0])]
    rights = [refs[3 * counts[0] + 2 * i :][:2] for i in range(counts[1])]
    keep_ref, send_ref, *scratch = refs[3 * counts[0] + 2 * counts[1] :]
    lefts_in, rights_in = scratch[: counts[0]], scratch[counts[0] : sum(counts)]
    total, sent, got = scratch[sum(counts) :]
    place = lax.axis_index("seq")
    partner = {"seq": place + 1 - 2 * (place % 2)}
    barrier = pltpu.get_barrier_semaphore()
    pl.semaphore_signal(barrier, inc=1, device_id=partner, device_id_type=pl.DeviceIdType.MESH)
    pl.semaphore_wait(barrier, 1)
    moves = []
    for (right, across), arrived in zip(rights, rights_in):
        moves += [(right, arrived.at[0]), (across, arrived.at[1])]
    for (own, beside, across), arrived in zip(lefts, lefts_in):
        rows = own.shape[0]
        moves += [(beside, arrived.at[0]), (across.at[pl.ds(rows, rows)], arrived.at[1])]
    copies = [
        pltpu.make_async_remote_copy(
            src_ref=source,
            dst_ref=target,
            send_sem=sent.at[i],
            recv_sem=got.at[i],
            device_id=partner,
            device_id_type=pl.DeviceIdType.MESH,
        )
        for i, (source, target) in enumerate(moves)
    ]
    for copy in copies:
        copy.start()
    unit = total.shape[0]
    pieces = []
    begin = 0
    for left, right, at in parts:
        columns = rights[right][0].shape[2]
        for piece in range(lefts[left][0].shape[0] // unit):
            rows = slice(piece * unit, (piece + 1) * unit)
            for first in range(0, columns, 512):
                chunk = slice(first, min(first + 512, columns))
                pieces.append((left, right, at, rows, chunk, slice(begin + chunk.start, begin + chunk.stop)))
            if columns % LANES:
                blank = slice(begin + columns, begin + -(-columns // LANES) * LANES)
                keep_ref[:, blank] = jnp.zeros((unit // 2, blank.stop - blank.start), bf16)
                send_ref[:, blank] = jnp.zeros((unit // 2, blank.stop - blank.start), bf16)
            begin += -(-columns // LANES) * LANES
    for left, right, at, rows, chunk, out in pieces:
        total[:, out] = jnp.dot(
            lefts[left][0][rows], rights[right][0][at, :, chunk], preferred_element_type=f32
        ) + jnp.dot(lefts[left][2][rows], rights[right][1][at, :, chunk], preferred_element_type=f32)
    for copy in copies:
        copy.wait()
    for left, right, at, rows, chunk, out in pieces:
        result = (
            total[:, out]
            + jnp.dot(lefts_in[left][0, rows], rights_in[right][0, at, :, chunk], preferred_element_type=f32)
            + jnp.dot(lefts_in[left][1, rows], rights_in[right][1, at, :, chunk], preferred_element_type=f32)
        )
        keep_ref[:, out] = result[: unit // 2].astype(bf16)
        send_ref[:, out] = result[unit // 2 :].astype(bf16)


def quarter_gradient(lefts, rights, parts, collective, order=()):
    unit = min(left[0].shape[0] for left in lefts)
    columns = sum(
        lefts[left][0].shape[0] // unit * -(-rights[right][0].shape[2] // LANES) * LANES
        for left, right, _ in parts
    )
    vmem = pl.BlockSpec(memory_space=pltpu.VMEM)
    counts = (len(lefts), len(rights))
    inputs = [array for group in lefts + rights for array in group]
    return pl.pallas_call(
        ignoring(functools.partial(quarter_kernel, parts, counts), len(inputs), len(order)),
        in_specs=[vmem] * len(inputs) + [pl.BlockSpec(memory_space=pl.ANY)] * len(order),
        out_specs=[vmem] * 2,
        out_shape=[jax.ShapeDtypeStruct((unit // 2, columns), bf16)] * 2,
        scratch_shapes=[pltpu.VMEM((2,) + left[0].shape, bf16) for left in lefts]
        + [pltpu.VMEM((2,) + right[0].shape, bf16) for right in rights]
        + [
            pltpu.VMEM((unit, columns), f32),
            pltpu.SemaphoreType.DMA((2 * sum(counts),)),
            pltpu.SemaphoreType.DMA((2 * sum(counts),)),
        ],
        compiler_params=pltpu.CompilerParams(
            vmem_limit_bytes=56 * 2**20, collective_id=collective, has_side_effects=True
        ),
        cost_estimate=taking(columns // 320),
        name="gradient",
    )(*inputs, *order)


def added(keep, received):
    total = keep.astype(f32) + received.astype(f32)
    half = total.shape[0] // 2
    return total[:half].astype(bf16), total[half:].astype(bf16)


def shared_rows(right):
    return right, seq_swap(right, 1)


class Gradient:
    def __init__(self, lefts, rights, parts, collective, order=()):
        self.lefts, self.parts, self.collective, self.order = lefts, parts, collective, order
        self.rights = [right if isinstance(right, tuple) else shared_rows(right) for right in rights]
        self.bits = lax.axis_size("seq").bit_length() - 1
        self.bit = 2
        self.total = None

    def start(self):
        self.received = seq_swap(self.send, self.bit)
        self.bit += 1

    def finish(self):
        if self.bit == 2:
            self.keep, self.send = quarter_gradient(
                self.lefts, self.rights, self.parts, self.collective, self.order
            )
        elif self.bit < self.bits:
            self.keep, self.send = added(self.keep, self.received)
        else:
            self.total = self.keep.astype(f32) + self.received.astype(f32)

    def results(self):
        unit = min(left[0].shape[0] for left in self.lefts)
        found, begin = [], 0
        for left, right, _ in self.parts:
            columns = self.rights[right][0].shape[2]
            blocks = []
            for _ in range(self.lefts[left][0].shape[0] // unit):
                blocks.append(self.total[:, begin : begin + columns])
                begin += -(-columns // LANES) * LANES
            found.append(blocks[0] if len(blocks) == 1 else jnp.concatenate(blocks, axis=0))
        return found


def after(value, *others):
    for other in others:
        value = value + (other.reshape(-1)[0] * 0).astype(value.dtype)
    return value


def finished(gradient):
    gradient.finish()
    arrays = [gradient.total] if gradient.total is not None else [gradient.keep, gradient.send]
    if gradient.total is None:
        gradient.start()
    return arrays


def ignoring(body, used, unused):
    return lambda *refs: body(*refs[:used], *refs[used + unused :])


def completed_all(gradients):
    while any(gradient.total is None for gradient in gradients):
        for gradient in gradients:
            if gradient.total is None:
                gradient.finish()
                if gradient.total is None:
                    gradient.start()


def column_chunks(value, chunks):
    width = value.shape[1] // lax.axis_size("wt")
    piece = -(-width // chunks // LANES) * LANES
    owners = cut_evenly(value, 1)
    return [
        to_own_columns(jnp.concatenate([owner[:, at : at + piece] for owner in owners], axis=1))
        for at in range(0, width, piece)
    ]


def lane_blocks(inner):
    blocks = inner // LANES
    return next(n for n in (5, 4, 3, 2, 1) if blocks % n == 0)

def cut_lanes(value):
    return [value[:, i * LANES : (i + 1) * LANES] for i in range(value.shape[1] // LANES)]

def spread(ref, tile, row, states):
    values = ref[tile, row : row + 1, :]
    return [jnp.broadcast_to(part, (states, LANES)) for part in cut_lanes(values)]


def advanced(size_ref, inject_ref, entry_ref, decay, tile, row, state):
    states = entry_ref.shape[1]
    into = entry_ref[tile * 8 + row]
    return tuple(
        jnp.exp2(size * rate) * old + inject * into
        for size, inject, rate, old in zip(
            spread(size_ref, tile, row, states), spread(inject_ref, tile, row, states), decay, state
        )
    )


def no_state(decay_ref):
    return tuple(jnp.zeros_like(part) for part in cut_lanes(decay_ref[...]))


def state_kernel(size_ref, inject_ref, entry_ref, decay_ref, last_ref):
    decay = cut_lanes(decay_ref[...])

    def tokens(tile, state):
        for row in range(8):
            state = advanced(size_ref, inject_ref, entry_ref, decay, tile, row, state)
        return state

    state = lax.fori_loop(0, size_ref.shape[0], tokens, no_state(decay_ref))
    last_ref[...] = jnp.concatenate(state, axis=1)


def output_kernel(size_ref, inject_ref, entry_ref, read_ref, decay_ref, begin_ref, out_ref):
    decay = cut_lanes(decay_ref[...])

    def tokens(tile, state):
        for row in range(8):
            state = advanced(size_ref, inject_ref, entry_ref, decay, tile, row, state)
            output = read_ref[tile * 8 + row]
            for i, part in enumerate(state):
                out_ref[tile, row : row + 1, i * LANES : (i + 1) * LANES] = jnp.sum(
                    output * part, axis=0, keepdims=True
                )
        return state

    lax.fori_loop(0, size_ref.shape[0], tokens, tuple(cut_lanes(begin_ref[...])))


def adjoint_kernel(size_ref, back_ref, read_ref, decay_ref, first_ref):
    states = decay_ref.shape[0]
    decay = cut_lanes(decay_ref[...])
    tiles = size_ref.shape[0]

    def tokens(turn, carry):
        tile = tiles - 1 - turn
        for row in reversed(range(8)):
            output = read_ref[tile * 8 + row]
            carry = tuple(
                jnp.exp2(size * rate) * (output * back + old)
                for size, back, rate, old in zip(
                    spread(size_ref, tile, row, states), spread(back_ref, tile, row, states), decay, carry
                )
            )
        return carry

    carry = lax.fori_loop(0, tiles, tokens, no_state(decay_ref))
    first_ref[...] = jnp.concatenate(carry, axis=1)


def gradient_kernel(
    size_ref,
    inject_ref,
    back_ref,
    entry_ref,
    read_ref,
    decay_ref,
    rate_ref,
    begin_ref,
    end_ref,
    through_ref,
    sized_ref,
    entry_back_ref,
    read_back_ref,
    decay_back_ref,
    prior_ref,
):
    states = decay_ref.shape[0]
    decay = cut_lanes(decay_ref[...])
    tiles = size_ref.shape[0]

    @pl.when(pl.program_id(0) == 0)
    def _():
        entry_back_ref[...] = jnp.zeros_like(entry_back_ref)
        read_back_ref[...] = jnp.zeros_like(read_back_ref)

    def forward(tile, state):
        for row in range(8):
            for i, part in enumerate(state):
                prior_ref[tile * 8 + row, :, i * LANES : (i + 1) * LANES] = part
            state = advanced(size_ref, inject_ref, entry_ref, decay, tile, row, state)
        return state

    last = lax.fori_loop(0, tiles, forward, tuple(cut_lanes(begin_ref[...])))

    def backward(turn, carry):
        tile = tiles - 1 - turn
        arriving, current, total = carry
        for row in reversed(range(8)):
            t = tile * 8 + row
            into = entry_ref[t]
            output = read_ref[t]
            sizes = spread(size_ref, tile, row, states)
            injects = spread(inject_ref, tile, row, states)
            backs = spread(back_ref, tile, row, states)
            entry_back = entry_back_ref[t]
            read_back = read_back_ref[t]
            new_arriving, new_current, new_total = [], [], []
            for k in range(len(decay)):
                lanes = slice(k * LANES, (k + 1) * LANES)
                prior = prior_ref[t, :, lanes]
                adjoint = output * backs[k] + arriving[k]
                leaving = jnp.exp2(sizes[k] * decay[k]) * adjoint
                weighted = leaving * prior
                through_ref[tile, row : row + 1, lanes] = jnp.sum(adjoint * into, axis=0, keepdims=True)
                sized_ref[tile, row : row + 1, lanes] = jnp.sum(
                    weighted * rate_ref[:, lanes], axis=0, keepdims=True
                )
                entry_back = entry_back + adjoint * injects[k]
                read_back = read_back + current[k] * backs[k]
                new_total.append(total[k] + weighted * sizes[k])
                new_arriving.append(leaving)
                new_current.append(prior)
            entry_back_ref[t] = entry_back
            read_back_ref[t] = read_back
            arriving, current, total = new_arriving, new_current, new_total
        return tuple(arriving), tuple(current), tuple(total)

    arriving = tuple(cut_lanes(end_ref[...]))
    _, _, total = lax.fori_loop(0, tiles, backward, (arriving, last, no_state(decay_ref)))
    decay_back_ref[...] = jnp.concatenate(total, axis=1)


def scan_call(body, name, token_args, wide_args, state_args, outs, scratch=False, flops=0, order=()):
    rows, inner = token_args[0].shape
    states = state_args[0].shape[0]
    width = lane_blocks(inner) * LANES
    token = pl.BlockSpec((rows // 8, 8, width), lambda i: (0, 0, i))
    wide = pl.BlockSpec((rows, states, LANES), lambda i: (0, 0, 0))
    state = pl.BlockSpec((states, width), lambda i: (0, i))
    kinds = {
        "token": (token, jax.ShapeDtypeStruct((rows // 8, 8, inner), f32)),
        "wide": (wide, jax.ShapeDtypeStruct((rows, states, LANES), f32)),
        "state": (state, jax.ShapeDtypeStruct((states, inner), f32)),
    }
    size = rows * states * inner
    results = pl.pallas_call(
        ignoring(body, len(token_args) + len(wide_args) + len(state_args), len(order)),
        grid=(inner // width,),
        in_specs=[token] * len(token_args)
        + [wide] * len(wide_args)
        + [state] * len(state_args)
        + [pl.BlockSpec(memory_space=pl.ANY)] * len(order),
        out_specs=[kinds[k][0] for k in outs],
        out_shape=[kinds[k][1] for k in outs],
        scratch_shapes=[pltpu.VMEM((rows, states, width), f32)] if scratch else [],
        compiler_params=pltpu.CompilerParams(vmem_limit_bytes=40 * 2**20),
        cost_estimate=taking(flops * 3 // 2),
        name=name,
    )(*[arg.reshape(rows // 8, 8, inner) for arg in token_args], *wide_args, *state_args, *order)
    return [r.reshape(rows, inner) if k == "token" else r for k, r in zip(outs, results)]


def entering_kernel(sign, hops, total_ref, part_ref, rate_ref, out_ref, totals, parts, totals_in, parts_in, sent, got):
    count = lax.axis_size("seq")
    place = lax.axis_index("seq")
    barrier = pltpu.get_barrier_semaphore()
    reaches = sorted({distance for _, distance in hops})
    for distance in reaches:
        pl.semaphore_signal(
            barrier,
            inc=1,
            device_id={"seq": (place + count - sign * distance) % count},
            device_id_type=pl.DeviceIdType.MESH,
        )
    pl.semaphore_wait(barrier, len(reaches))

    def send(turn):
        buffer, distance = hops[turn]
        copies = [
            pltpu.make_async_remote_copy(
                src_ref=source,
                dst_ref=target,
                send_sem=sent.at[turn, i],
                recv_sem=got.at[turn, i],
                device_id={"seq": (place + count + sign * distance) % count},
                device_id_type=pl.DeviceIdType.MESH,
            )
            for i, (source, target) in enumerate(
                [(totals.at[buffer], totals_in.at[turn]), (parts.at[buffer], parts_in.at[turn])]
            )
        ]
        for copy in copies:
            copy.start()
        return copies

    def joined(near, far):
        (total, part), (far_total, far_part) = near, far
        passed = [
            jnp.exp2(total[k : k + 1] * rate_ref[:, k * LANES : (k + 1) * LANES])
            for k in range(total.shape[0])
        ]
        return total + far_total, jnp.concatenate(passed, axis=1) * far_part + part

    def received(turn, copies):
        for copy in copies:
            copy.wait()
        distance = hops[turn][1]
        there = place >= distance if sign > 0 else place < count - distance
        return jnp.where(there, totals_in[turn], 0.0), jnp.where(there, parts_in[turn].astype(f32), 0.0)

    totals[0] = total_ref[...]
    parts[0] = part_ref[...].astype(bf16)
    first = [send(0), send(1)]
    state = joined(received(0, first[0]), received(1, first[1]))
    for turn in range(2, len(hops)):
        buffer = hops[turn][0]
        totals[buffer] = state[0]
        parts[buffer] = state[1].astype(bf16)
        state = joined(state, received(turn, send(turn)))
    out_ref[...] = state[1]


def entering(total, part, rate, reverse, order):
    count = lax.axis_size("seq")
    states, inner = part.shape
    total = total.reshape(-1, LANES)
    hops = [(0, 1), (0, 2)] + [(bit, 1 << bit) for bit in range(1, count.bit_length() - 1)]
    buffers = len(hops) - 1
    vmem = pl.BlockSpec(memory_space=pltpu.VMEM)
    return pl.pallas_call(
        ignoring(functools.partial(entering_kernel, -1 if reverse else 1, hops), 3, len(order)),
        in_specs=[vmem] * 3 + [pl.BlockSpec(memory_space=pl.ANY)] * len(order),
        out_specs=vmem,
        out_shape=jax.ShapeDtypeStruct(part.shape, f32),
        scratch_shapes=[
            pltpu.VMEM((buffers,) + total.shape, f32),
            pltpu.VMEM((buffers, states, inner), bf16),
            pltpu.VMEM((len(hops),) + total.shape, f32),
            pltpu.VMEM((len(hops), states, inner), bf16),
            pltpu.SemaphoreType.DMA((len(hops), 2)),
            pltpu.SemaphoreType.DMA((len(hops), 2)),
        ],
        compiler_params=pltpu.CompilerParams(
            vmem_limit_bytes=24 * 2**20, collective_id=10 if reverse else 9, has_side_effects=True
        ),
        cost_estimate=taking(24),
        name="entering",
    )(total, part, rate, *order)


def summed_everywhere(values):
    for axis in ("wt", "seq"):
        count = lax.axis_size(axis)
        bit = 1
        while bit < count:
            received = lax.ppermute(values, axis, [(i, i ^ bit) for i in range(count)])
            values = (values.astype(f32) + received.astype(f32)).astype(values.dtype)
            bit *= 2
    return values


def product(left, right):
    return jnp.dot(left, right, preferred_element_type=jnp.float32)


def left_product(left, right):
    return lax.dot_general(
        left, right, (((0,), (0,)), ((), ())), preferred_element_type=jnp.float32
    )


def right_product(left, right):
    return lax.dot_general(
        left, right, (((1,), (1,)), ((), ())), preferred_element_type=jnp.float32
    )


def transposed_dot(left, right):
    return lax.dot_general(left, right, (((0,), (0,)), ((), ())), preferred_element_type=f32)


def heads_beside(value):
    heads = value.shape[0] // HEAD_SIZE
    return jnp.concatenate(
        [value[h * HEAD_SIZE : (h + 1) * HEAD_SIZE] for h in range(heads)], axis=1
    )


def store_heads(ref, value):
    rows = ref.shape[1]
    for h in range(ref.shape[0] // HEAD_SIZE):
        ref[h * HEAD_SIZE : (h + 1) * HEAD_SIZE, :] = value[:, h * rows : (h + 1) * rows].astype(ref.dtype)


def chance_table(query, keys, bias):
    heads = query.shape[1] // bias.shape[1]
    scores = transposed_dot(keys, query) + jnp.concatenate([bias] * heads, axis=1)
    raised = jnp.exp(scores - jnp.max(scores, axis=0, keepdims=True))
    return raised * (1.0 / jnp.sum(raised, axis=0, keepdims=True))


def attend_kernel(query_ref, near_ref, bias_ref, out_ref):
    query = heads_beside(query_ref[...]) * bf16(0.125)
    chances = chance_table(query, near_ref[0], bias_ref[...]).astype(bf16)
    store_heads(out_ref, jnp.dot(near_ref[1], chances, preferred_element_type=f32))


def attend_back_kernel(query_ref, near_ref, back_ref, bias_ref, query_back_ref, kept_ref, sent_ref):
    query = heads_beside(query_ref[...]) * bf16(0.125)
    back = heads_beside(back_ref[...])
    weights = chance_table(query, near_ref[0], bias_ref[...])
    values_back = right_product(back, weights.astype(bf16))
    delta = transposed_dot(near_ref[1], back)
    weighted = weights * delta
    scores_back = (weighted - weights * jnp.sum(weighted, axis=0, keepdims=True)).astype(bf16)
    store_heads(query_back_ref, jnp.dot(near_ref[0], scores_back, preferred_element_type=f32) * 0.125)
    half = kept_ref.shape[2]
    for place, near_back in enumerate((right_product(query, scores_back), values_back)):
        kept_ref[place] = near_back[:, :half]
        sent_ref[place] = near_back[:, half:].astype(bf16)


def attention_call(body, name, wide, near, bias, outs, flops, order=()):
    span, rows = bias.shape
    key_heads = near.shape[1] // HEAD_SIZE
    width = wide[0].shape[0] // key_heads
    wide_spec = pl.BlockSpec((width, rows), lambda k: (k, 0))
    near_spec = lambda size: pl.BlockSpec((2, HEAD_SIZE, size), lambda k: (0, k, 0))
    half = near.shape[:2] + (span // 2,)
    kinds = {
        "wide": (wide_spec, jax.ShapeDtypeStruct(wide[0].shape, bf16)),
        "kept": (near_spec(span // 2), jax.ShapeDtypeStruct(half, f32)),
        "sent": (near_spec(span // 2), jax.ShapeDtypeStruct(half, bf16)),
    }
    return pl.pallas_call(
        ignoring(body, len(wide) + 2, len(order)),
        grid=(key_heads,),
        in_specs=[wide_spec, near_spec(span)]
        + [wide_spec] * (len(wide) - 1)
        + [pl.BlockSpec((span, rows), lambda k: (0, 0))]
        + [pl.BlockSpec(memory_space=pl.ANY)] * len(order),
        out_specs=[kinds[k][0] for k in outs],
        out_shape=[kinds[k][1] for k in outs],
        compiler_params=pltpu.CompilerParams(vmem_limit_bytes=56 * 2**20),
        cost_estimate=taking(flops * 4),
        name=name,
    )(wide[0], near, *wide[1:], bias, *order)


def outer_product(left, right):
    return lax.dot_general(left, right, (((0,), (1,)), ((), ())), preferred_element_type=f32)


def inverse_norm(value):
    return lax.rsqrt(jnp.mean(value * value, axis=-1, keepdims=True) + epsilon)


def norm_back(value, scale, incoming):
    return scale * incoming - scale * scale * scale * value * jnp.mean(
        incoming * value, axis=-1, keepdims=True
    )


def silu_slope(value):
    sigma = jax.nn.sigmoid(value)
    return sigma * (1.0 + value * (1.0 - sigma))


def gather_columns(own):
    count = lax.axis_size("wt")
    turned = own.T
    return in_order([turned] + [from_ahead(turned, k) for k in range(1, count)], 0)


def feed_kernel(
    columns,
    second_ref,
    back_ref,
    gate_ref,
    up_ref,
    down_ref,
    out_ref,
    second_back_ref,
    activated_ref,
    hidden_back_ref,
    out_sum,
    second_back_sum,
):
    width = gate_ref.shape[1]
    step, last = pl.program_id(0), pl.num_programs(0) - 1

    def part(width, begin):
        gate, up, down = (ref[:, :width] for ref in (gate_ref, up_ref, down_ref))
        gate_raw = product(second_ref[...], gate)
        up_raw = product(second_ref[...], up)
        act_back = product(back_ref[...], down)
        sigma = jax.nn.sigmoid(gate_raw)
        swish = gate_raw * sigma
        activated = (swish * up_raw).astype(bf16)
        gate_back = (act_back * up_raw * (sigma * (1.0 + gate_raw * (1.0 - sigma)))).astype(bf16)
        up_back = (act_back * swish).astype(bf16)
        activated_ref[:, :width] = activated
        hidden_back_ref[0, :, :width] = gate_back
        hidden_back_ref[1, :, :width] = up_back
        out = right_product(down, activated)
        second_back = right_product(gate, gate_back) + right_product(up, up_back)
        if begin:
            out_sum[...] = out
            second_back_sum[...] = second_back
        else:
            out_sum[...] += out
            second_back_sum[...] += second_back

    pl.when(step == 0)(lambda: part(width, True))
    pl.when((step > 0) & (step < last))(lambda: part(width, False))

    @pl.when(step == last)
    def _():
        left = columns - (-(-columns // width) - 1) * width
        part(left, False)
        if left < width:
            activated_ref[:, left:] = jnp.zeros((activated_ref.shape[0], width - left), bf16)
            hidden_back_ref[:, :, left:] = jnp.zeros((2, activated_ref.shape[0], width - left), bf16)
        out_ref[...] = out_sum[...].T
        second_back_ref[...] = second_back_sum[...].T


def feed_block(second, back, gate, up, down, order, width=512):
    rows, model = second.shape
    columns = gate.shape[1]
    padded = -(-columns // LANES) * LANES
    whole = pl.BlockSpec((rows, model), lambda i: (0, 0))
    weight = pl.BlockSpec((model, width), lambda i: (0, i))
    hidden = pl.BlockSpec((rows, width), lambda i: (0, i))
    return pl.pallas_call(
        ignoring(functools.partial(feed_kernel, columns), 5, len(order)),
        grid=(-(-columns // width),),
        in_specs=[whole, whole, weight, weight, weight]
        + [pl.BlockSpec(memory_space=pl.ANY)] * len(order),
        out_specs=[whole, whole, hidden, pl.BlockSpec((2, rows, width), lambda i: (0, 0, i))],
        out_shape=[jax.ShapeDtypeStruct((rows, model), f32)] * 2
        + [jax.ShapeDtypeStruct(shape, bf16) for shape in ((rows, padded), (2, rows, padded))],
        scratch_shapes=[pltpu.VMEM((model, rows), f32)] * 2,
        compiler_params=pltpu.CompilerParams(vmem_limit_bytes=48 * 2**20),
        cost_estimate=taking(22),
        name="feed",
    )(second, back, gate, up, down, *order)


def per_device(
    tokens,
    segment_ids,
    cotangent,
    norm_gain,
    query_weight,
    key_weight,
    value_weight,
    head_weight,
    input_weight,
    filter_weight,
    filter_bias,
    select_weight,
    step_weight,
    step_offset,
    decay_log,
    direct_skip_weight,
    mixer_weight,
    attend_gain,
    state_gain,
    feed_gain,
    gate_weight,
    up_weight,
    down_weight,
):
    rows = tokens.shape[1]
    model = tokens.shape[2]
    inner = filter_weight.shape[1]
    kernel = filter_weight.shape[0]
    states = decay_log.shape[0]
    start = lax.axis_index("seq") * rows
    whole_segment = segment_ids[0]
    padded_segment = jnp.concatenate([jnp.full((WINDOW,), -1, jnp.int32), whole_segment])
    segment = lax.dynamic_slice_in_dim(whole_segment, start, rows)
    inputs = tokens[0].astype(jnp.float32)
    upstream = cotangent[0].astype(jnp.float32)
    both_tokens = gather_tokens(tokens[0])
    select_full = gather_columns(select_weight)
    step_full = gather_columns(step_weight)
    rank = step_full.shape[0]
    first_scale = inverse_norm(inputs)
    both_inputs = both_tokens.astype(jnp.float32)
    both_normed = (both_inputs * inverse_norm(both_inputs) * norm_gain).astype(jnp.bfloat16)
    normed_shared = shared_features(both_normed, model)
    pairs = jnp.stack(
        [outer_product(weight, both_normed).astype(bf16) for weight in (key_weight, value_weight)]
    )
    pairs = to_own_tokens(pairs, 2, 1)
    entered = to_own_tokens(product(both_normed, input_weight).astype(jnp.bfloat16))
    both_back = gather_tokens(after(cotangent[0], entered))
    back_shared = shared_features(both_back, model)
    query = to_own_tokens(outer_product(query_weight, both_normed).astype(jnp.bfloat16), 1, 0)
    hops = -(-WINDOW // (4 * rows))
    near = jnp.concatenate(
        [pairs] + [passed_along(pairs, "seq", 4 * hop) for hop in range(1, hops + 1)], axis=2
    )
    seq_place = lax.axis_index("seq")
    block_places = jnp.stack(
        [(seq_place ^ other) - 4 * hop for other in (0, 2, 1, 3) for hop in range(hops + 1)]
    )
    near_place = (block_places[:, None] * rows + jnp.arange(rows, dtype=jnp.int32)[None, :]).reshape(-1)
    near_segment = jnp.where(
        block_places[:, None] >= 0,
        jnp.take(whole_segment.reshape(-1, rows), jnp.maximum(block_places, 0), axis=0),
        -1,
    ).reshape(-1)
    distance = start + jnp.arange(rows, dtype=jnp.int32)[None, :] - near_place[:, None]
    allowed = (distance >= 0) & (distance < WINDOW) & (segment[None, :] == near_segment[:, None])
    bias = jnp.where(allowed, 0.0, masked)
    inner_rows = entered[:, :inner]
    select_full = after(select_full, entered)
    step_full = after(step_full, entered)
    gate_input = entered[:, inner:].astype(jnp.float32)
    before = passed_along(inner_rows[rows - kernel + 1 :], "seq", 1)
    extended = jnp.concatenate([before, inner_rows], axis=0).astype(jnp.float32)
    edge_segment = lax.dynamic_slice_in_dim(
        padded_segment, start + WINDOW - kernel + 1, rows + kernel - 1
    )
    taps = []
    sames = []
    filtered = filter_bias + jnp.zeros((rows, inner), jnp.float32)
    for tap in range(kernel):
        begin = kernel - 1 - tap
        same = (edge_segment[begin : begin + rows] == segment).astype(jnp.float32)
        kept_rows = extended[begin : begin + rows] * same[:, None]
        taps.append(kept_rows)
        sames.append(same)
        filtered = filtered + filter_weight[tap] * kept_rows
    smoothed = (filtered * jax.nn.sigmoid(filtered)).astype(jnp.bfloat16)
    scan_input_rows = smoothed.astype(jnp.float32)
    smoothed_shared = shared_features(smoothed, model)
    projected = right_product(smoothed, select_full)
    step_low = projected[:, :rank].astype(jnp.bfloat16)
    step_low_shared = shared_rows(step_low[None])
    entry = projected[:, rank : rank + states]
    read = projected[:, rank + states :]
    unsquashed_step = product(step_low, step_full) + step_offset
    step = jnp.log1p(jnp.exp(unsquashed_step))
    previous = lax.dynamic_slice_in_dim(padded_segment, start + WINDOW - 1, rows)
    hold = (previous == segment).astype(jnp.float32)
    decay = -jnp.exp(decay_log)
    rate = decay * LOG2E
    size = jnp.where(hold[:, None] == 0.0, 1e30, step)
    inject = step * scan_input_rows
    entry_wide = jnp.broadcast_to(entry[:, :, None], (rows, states, LANES))
    read_wide = jnp.broadcast_to(read[:, :, None], (rows, states, LANES))
    total = jnp.sum(size, axis=0)
    (last,) = scan_call(state_kernel, "scan_state", [size, inject], [entry_wide], [rate], ["state"], flops=4, order=[normed_shared[2]])
    for bit in (1, 0):
        near = jnp.concatenate([near, seq_swap(near, bit)], axis=2)
    (attended,) = attention_call(attend_kernel, "attend", [query], near, bias, ["wide"], 2, order=[back_shared[2]])
    begin_state = entering(total, last, rate, False, [])
    both_attended = gather_tokens(attended, 1)
    attended_shared = shared_features(both_attended, model, turned=False)
    head_out = to_own_tokens(left_product(both_attended, head_weight).astype(bf16)).astype(f32)
    (scanned,) = scan_call(
        output_kernel, "scan_output", [size, inject], [entry_wide, read_wide], [rate, begin_state], ["token"], flops=6, order=[both_back, attended, smoothed_shared[2], step_low_shared[1]]
    )
    scan_result_rows = scanned + direct_skip_weight * scan_input_rows
    sigma_input = jax.nn.sigmoid(gate_input)
    silu_input = gate_input * sigma_input
    gated = (scan_result_rows * silu_input).astype(jnp.bfloat16)
    both_gated = gather_tokens(gated)
    gated_shared = shared_features(both_gated, model)
    branch = to_own_tokens(product(both_gated, mixer_weight).astype(jnp.bfloat16)).astype(f32)
    head_scale = inverse_norm(head_out)
    branch_scale = inverse_norm(branch)
    hidden = inputs + 0.5 * (
        head_out * head_scale * attend_gain + branch * branch_scale * state_gain
    )
    second_scale = inverse_norm(hidden)
    second = (hidden * second_scale * feed_gain).astype(jnp.bfloat16)
    both_second = gather_tokens(second)
    feed_part, second_part, activated, hidden_back = feed_block(
        both_second,
        both_back,
        gate_weight,
        up_weight,
        down_weight,
        [attended_shared[2], gated_shared[2]],
    )
    second_shared = shared_features(both_second, model)
    delta_second = summed_tokens(second_part)
    feed_out = summed_tokens(feed_part)
    result = (hidden + feed_out).astype(jnp.bfloat16)
    feed_sum = jnp.sum(delta_second * hidden * second_scale, axis=0)
    delta_hidden = upstream + norm_back(hidden, second_scale, delta_second * feed_gain)
    half = 0.5 * delta_hidden
    attend_sum = jnp.sum(half * head_out * head_scale, axis=0)
    state_sum = jnp.sum(half * branch * branch_scale, axis=0)
    delta_head = norm_back(head_out, head_scale, half * attend_gain).astype(jnp.bfloat16)
    delta_branch = norm_back(branch, branch_scale, half * state_gain).astype(jnp.bfloat16)
    both_deltas = to_own_columns(jnp.stack([delta_head, delta_branch]), 1, 2)
    both_delta_head, both_delta_branch = both_deltas[0], both_deltas[1]
    delta_gated = summed_tokens(right_product(both_delta_branch, mixer_weight))
    delta_attended = summed_tokens(right_product(head_weight, both_delta_head), 1).astype(bf16)
    delta_scan_output = delta_gated * silu_input
    delta_gate = (delta_gated * scan_result_rows * silu_slope(gate_input)).astype(jnp.bfloat16)
    skip_sum = jnp.sum(delta_scan_output * scan_input_rows, axis=0)
    hidden_shared = shared_rows(hidden_back)
    (first,) = scan_call(
        adjoint_kernel,
        "scan_adjoint",
        [size, delta_scan_output],
        [read_wide],
        [rate],
        ["state"],
        flops=4,
        order=[hidden_shared[1]],
    )
    end_state = entering(total, first, rate, True, [])
    middle_sums = Gradient(
        [second_shared, attended_shared, gated_shared],
        [hidden_shared, both_deltas],
        [(0, 0, 0), (0, 0, 1), (1, 1, 0), (2, 1, 1)],
        2,
        order=[end_state],
    )
    through, sized, entry_back, read_back, decay_acc = scan_call(
        gradient_kernel,
        "scan_gradient",
        [size, inject, delta_scan_output],
        [entry_wide, read_wide],
        [rate, decay, begin_state, end_state],
        ["token", "token", "wide", "wide", "state"],
        scratch=True,
        flops=20,
        order=finished(middle_sums),
    )
    down = Gradient([back_shared], [after(activated, end_state)[None]], [(0, 0, 0)], 1, order=[through])
    delta_query, delta_near, sent_near = attention_call(
        attend_back_kernel,
        "attend_back",
        [query, delta_attended],
        near,
        bias,
        ["wide", "kept", "sent"],
        5,
        order=[through],
    )
    delta_near = delta_near + seq_swap(sent_near, 0).astype(f32)
    middle = delta_near.shape[2] // 2
    received = seq_swap(delta_near[:, :, middle:].astype(bf16), 1)
    delta_near = delta_near[:, :, :middle] + received.astype(f32)
    delta_pairs = delta_near[:, :, :rows]
    for hop in range(1, hops + 1):
        piece = delta_near[:, :, hop * rows : (hop + 1) * rows].astype(bf16)
        delta_pairs = delta_pairs + passed_along(piece, "seq", -4 * hop).astype(f32)
    delta_pairs = delta_pairs.astype(jnp.bfloat16)
    both_qkv = jnp.concatenate(
        [
            to_own_columns(delta_query, 1, 0),
            to_own_columns(delta_pairs[0], 1, 0),
            to_own_columns(delta_pairs[1], 1, 0),
        ],
        axis=0,
    ).T
    qkv_shared = shared_rows(both_qkv[None])
    decay_sum = decay_acc * decay
    delta_scan_input = delta_scan_output * direct_skip_weight + through * step
    delta_unsquashed_step = (sized + through * scan_input_rows) * jax.nn.sigmoid(unsquashed_step)
    offset_sum = jnp.sum(delta_unsquashed_step, axis=0)
    raw_low = delta_unsquashed_step.astype(jnp.bfloat16)
    delta_lowrank_step = right_product(raw_low, step_full)
    delta_projected = jnp.concatenate(
        [
            delta_lowrank_step,
            jnp.sum(entry_back, axis=-1),
            jnp.sum(read_back, axis=-1),
        ],
        axis=1,
    ).astype(jnp.bfloat16)
    delta_scan_input = delta_scan_input + product(delta_projected, select_full)
    delta_filtered = delta_scan_input * silu_slope(filtered)
    bias_sum = jnp.sum(delta_filtered, axis=0)
    filter_sums = jnp.stack([jnp.sum(delta_filtered * kept_rows, axis=0) for kept_rows in taps])
    shares = [delta_filtered * filter_weight[tap] * sames[tap][:, None] for tap in range(kernel)]
    leaving = jnp.stack(
        [
            sum(shares[tap][tap - back] for tap in range(back, kernel))
            for back in range(kernel - 1, 0, -1)
        ]
    )
    arrived = passed_along(leaving.astype(jnp.bfloat16), "seq", -1).astype(jnp.float32)
    delta_inner = sum(jnp.pad(share[tap:], ((0, tap), (0, 0))) for tap, share in enumerate(shares))
    delta_inner = delta_inner + jnp.pad(arrived, ((rows - kernel + 1, 0), (0, 0)))
    delta_entered = jnp.concatenate([delta_inner.astype(jnp.bfloat16), delta_gate], axis=1)
    both_entered = column_chunks(delta_entered, 4)
    widths = (query_weight.shape[1], key_weight.shape[1], value_weight.shape[1])
    cuts = (0, widths[0], widths[0] + widths[1], sum(widths))
    delta_normed = right_product(jnp.concatenate(both_entered, axis=1), input_weight)
    for place, weight in enumerate((query_weight, key_weight, value_weight)):
        delta_normed = delta_normed + right_product(both_qkv[:, cuts[place] : cuts[place + 1]], weight)
    delta_normed = summed_tokens(delta_normed)
    norm_sum = jnp.sum(delta_normed * inputs * first_scale, axis=0)
    delta_tokens = delta_hidden + norm_back(inputs, first_scale, delta_normed * norm_gain)
    raw_shared = shared_features(raw_low, model, order=[both_entered[0]])
    late_sums = Gradient(
        [normed_shared, smoothed_shared, raw_shared],
        [qkv_shared, after(delta_projected, both_entered[0])[None], step_low_shared],
        [(0, 0, 0), (1, 1, 0), (2, 2, 0)],
        3,
        order=[both_entered[0]],
    )
    middle_placed = finished(middle_sums)
    input_sums = [
        Gradient([normed_shared], [part[None]], [(0, 0, 0)], 4 if part.shape == both_entered[0].shape else 5, middle_placed)
        for part in both_entered
    ]
    for gradient in input_sums:
        finished(gradient)
    input_placed = input_sums[-1].keep
    late_sums.order = [input_placed]
    completed_all(input_sums + [late_sums, down, middle_sums])
    qkv_gradient, select_sum, step_sum = late_sums.results()
    query_gradient, key_gradient, value_gradient = (
        qkv_gradient[:, cuts[place] : cuts[place + 1]] for place in range(3)
    )
    select_gradient, step_gradient = own_columns_sums((select_sum, step_sum))
    input_gradient = jnp.concatenate([gradient.results()[0] for gradient in input_sums], axis=1)
    gate_gradient, up_gradient, head_gradient, mixer_gradient = middle_sums.results()
    (down_gradient,) = down.results()
    hidden_width = gate_weight.shape[1]
    gate_gradient, up_gradient, down_gradient = (
        gradient[:, :hidden_width] for gradient in (gate_gradient, up_gradient, down_gradient)
    )
    early = jnp.concatenate(
        [
            decay_sum,
            filter_sums,
            jnp.stack([bias_sum, offset_sum, skip_sum, jnp.concatenate([attend_sum, state_sum])]),
            jnp.concatenate([feed_sum, norm_sum])[None],
        ],
        axis=0,
    )
    early_total = summed_everywhere(after(early, input_placed).astype(bf16)).astype(f32)
    decay_total = early_total[:states]
    filter_total = early_total[states : states + kernel]
    bias_total, offset_total, skip_total, pair_total, last_total = early_total[states + kernel :]
    attend_total, state_total = pair_total[:model], pair_total[model:]
    feed_total, norm_total = last_total[:model], last_total[model:]
    return (
        result[None],
        delta_tokens[None],
        norm_total,
        query_gradient,
        key_gradient,
        value_gradient,
        head_gradient,
        input_gradient,
        filter_total,
        bias_total,
        select_gradient,
        step_gradient,
        offset_total,
        decay_total,
        skip_total,
        mixer_gradient,
        attend_total,
        state_total,
        feed_total,
        gate_gradient,
        up_gradient,
        down_gradient,
    )


def solution(mesh):
    placed = (
        P("wt", "seq", None),
        P("wt", None),
        P("wt", "seq", None),
        P(),
        P(None, "wt"),
        P(None, "wt"),
        P(None, "wt"),
        P(None, "wt"),
        P(None, "wt"),
        P(),
        P(),
        P(None, "wt"),
        P(None, "wt"),
        P(),
        P(),
        P(),
        P(None, "wt"),
        P(),
        P(),
        P(),
        P(None, "wt"),
        P(None, "wt"),
        P(None, "wt"),
    )
    return jax.shard_map(
        per_device,
        mesh=mesh,
        in_specs=placed,
        out_specs=(
            P("wt", "seq", None),
            P("wt", "seq", None),
            P(),
            P("seq", "wt"),
            P("seq", "wt"),
            P("seq", "wt"),
            P("seq", "wt"),
            P("seq", "wt"),
            P(),
            P(),
            P("seq", "wt"),
            P("seq", "wt"),
            P(),
            P(),
            P(),
            P("seq", "wt"),
            P(),
            P(),
            P(),
            P("seq", "wt"),
            P("seq", "wt"),
            P("seq", "wt"),
        ),
        check_vma=False,
    )
```

```python
import functools

import jax
import jax.numpy as jnp
from jax import lax
from jax.experimental import pallas as pl
from jax.experimental.pallas import tpu as pltpu
from jax.sharding import PartitionSpec as P

HEAD_SIZE = 64
WINDOW = 1024


epsilon = 1e-06
masked = -1e30
bf16 = jnp.bfloat16
f32 = jnp.float32
LANES = 128
LOG2E = 1.4426950408889634


def passed_along(block, axis, distance):
    devices = range(lax.axis_size(axis))
    route = [(i - distance, i) for i in devices if i - distance in devices]
    return lax.ppermute(block, axis, route)


def from_ahead(block, distance):
    count = lax.axis_size("wt")
    return lax.ppermute(block, "wt", [((i + distance) % count, i) for i in range(count)])


def picked(blocks, index):
    result = blocks[0]
    for place in range(1, len(blocks)):
        result = jnp.where(index == place, blocks[place], result)
    return result


def gather_tokens(rows, axis=0):
    count = lax.axis_size("wt")
    return jnp.concatenate([rows] + [from_ahead(rows, k) for k in range(1, count)], axis=axis)


def swapped(blocks):
    count = len(blocks)
    return [blocks[0]] + [from_ahead(blocks[count - k], k) for k in range(1, count)]


def in_order(received, axis):
    place = lax.axis_index("wt")
    count = len(received)
    return jnp.concatenate([picked(received, (a - place) % count) for a in range(count)], axis=axis)


def cut_evenly(value, axis):
    return jnp.split(value, lax.axis_size("wt"), axis=axis)


def to_own_tokens(value, tokens=0, columns=1):
    return in_order(swapped(cut_evenly(value, tokens)), columns)


def to_own_columns(value, tokens=0, columns=1):
    count = lax.axis_size("wt")
    place = lax.axis_index("wt")
    owners = cut_evenly(value, columns)
    blocks = [picked(owners, (place + k) % count) for k in range(count)]
    return jnp.concatenate(swapped(blocks), axis=tokens)


def summed_tokens(value, tokens=0):
    blocks = cut_evenly(value, tokens)
    received = swapped([blocks[0]] + [b.astype(bf16) for b in blocks[1:]])
    total = received[0]
    for block in received[1:]:
        total = total + block.astype(f32)
    return total


def own_columns_sums(values):
    count = lax.axis_size("wt")
    place = lax.axis_index("wt")
    widths = [value.shape[1] // count for value in values]
    owners = [jnp.concatenate(parts, axis=1) for parts in zip(*(cut_evenly(value, 1) for value in values))]
    total = sum(swapped([picked(owners, (place + k) % count) for k in range(count)]))
    return [total[:, sum(widths[:i]) : sum(widths[: i + 1])] for i in range(len(widths))]


def taking(microseconds):
    return pl.CostEstimate(flops=0, transcendentals=0, bytes_accessed=microseconds * 30000)


def seq_swap(block, bit):
    count = lax.axis_size("seq")
    return lax.ppermute(block, "seq", [(i, i ^ (1 << bit)) for i in range(count)])


def reversed_bits(value, bits):
    return sum(((value >> bit) & 1) << (bits - 1 - bit) for bit in range(bits))


def arrange_kernel(turned, pieces, place_ref, left_ref, own_ref, across_ref, beside_ref, groups_ref, taken_ref):
    count, _, _ = groups_ref.shape
    bits = count.bit_length() - 1
    left = left_ref[...].astype(f32)
    left = left.T if turned else left
    group = left.shape[0] // count
    for r in range(count):
        groups_ref[r, :group, :] = left[r * group : (r + 1) * group]
    quarter, unit = own_ref.shape[0], group // pieces
    for r in range(count):
        for piece in range(pieces):
            begin = r // (count // 4) * quarter + piece * (quarter // pieces) + r % (count // 4) * unit
            taken_ref[begin : begin + unit, :] = groups_ref[
                place_ref[0] ^ reversed_bits(r, bits), piece * unit : (piece + 1) * unit, :
            ]
    own_ref[...] = taken_ref[:quarter].astype(bf16)
    across_ref[:quarter] = taken_ref[quarter : 2 * quarter].astype(bf16)
    across_ref[quarter:] = taken_ref[3 * quarter :].astype(bf16)
    beside_ref[...] = taken_ref[2 * quarter : 3 * quarter].astype(bf16)


def shared_features(left, model, turned=True, order=()):
    count = lax.axis_size("seq")
    tokens, features = left.shape if turned else left.shape[::-1]
    quarter = features // 4
    place = lax.axis_index("seq").astype(jnp.int32).reshape(1)
    whole = lambda shape: pl.BlockSpec(shape, lambda i, place: (0, 0))
    shapes = [(quarter, tokens), (2 * quarter, tokens), (quarter, tokens)]
    own, across, beside = pl.pallas_call(
        ignoring(functools.partial(arrange_kernel, turned, features // model), 2, len(order)),
        grid_spec=pltpu.PrefetchScalarGridSpec(
            num_scalar_prefetch=1,
            grid=(1,),
            in_specs=[whole(left.shape)] + [pl.BlockSpec(memory_space=pl.ANY)] * len(order),
            out_specs=[whole(shape) for shape in shapes],
            scratch_shapes=[
                pltpu.VMEM((count, -(-features // count // 8) * 8, tokens), f32),
                pltpu.VMEM((features, tokens), f32),
            ],
        ),
        out_shape=[jax.ShapeDtypeStruct(shape, bf16) for shape in shapes],
        compiler_params=pltpu.CompilerParams(vmem_limit_bytes=32 * 2**20),
        cost_estimate=taking(2),
        name="arrange",
    )(place, left, *order)
    return own, beside, seq_swap(across, 1)


def quarter_kernel(parts, counts, *refs):
    lefts = [refs[3 * i : 3 * i + 3] for i in range(counts[0])]
    rights = [refs[3 * counts[0] + 2 * i :][:2] for i in range(counts[1])]
    keep_ref, send_ref, *scratch = refs[3 * counts[0] + 2 * counts[1] :]
    lefts_in, rights_in = scratch[: counts[0]], scratch[counts[0] : sum(counts)]
    total, sent, got = scratch[sum(counts) :]
    place = lax.axis_index("seq")
    partner = {"seq": place + 1 - 2 * (place % 2)}
    barrier = pltpu.get_barrier_semaphore()
    pl.semaphore_signal(barrier, inc=1, device_id=partner, device_id_type=pl.DeviceIdType.MESH)
    pl.semaphore_wait(barrier, 1)
    moves = []
    for (right, across), arrived in zip(rights, rights_in):
        moves += [(right, arrived.at[0]), (across, arrived.at[1])]
    for (own, beside, across), arrived in zip(lefts, lefts_in):
        rows = own.shape[0]
        moves += [(beside, arrived.at[0]), (across.at[pl.ds(rows, rows)], arrived.at[1])]
    copies = [
        pltpu.make_async_remote_copy(
            src_ref=source,
            dst_ref=target,
            send_sem=sent.at[i],
            recv_sem=got.at[i],
            device_id=partner,
            device_id_type=pl.DeviceIdType.MESH,
        )
        for i, (source, target) in enumerate(moves)
    ]
    for copy in copies:
        copy.start()
    unit = total.shape[0]
    pieces = []
    begin = 0
    for left, right, at in parts:
        columns = rights[right][0].shape[2]
        for piece in range(lefts[left][0].shape[0] // unit):
            rows = slice(piece * unit, (piece + 1) * unit)
            for first in range(0, columns, 512):
                chunk = slice(first, min(first + 512, columns))
                pieces.append((left, right, at, rows, chunk, slice(begin + chunk.start, begin + chunk.stop)))
            if columns % LANES:
                blank = slice(begin + columns, begin + -(-columns // LANES) * LANES)
                keep_ref[:, blank] = jnp.zeros((unit // 2, blank.stop - blank.start), bf16)
                send_ref[:, blank] = jnp.zeros((unit // 2, blank.stop - blank.start), bf16)
            begin += -(-columns // LANES) * LANES
    for left, right, at, rows, chunk, out in pieces:
        total[:, out] = jnp.dot(
            lefts[left][0][rows], rights[right][0][at, :, chunk], preferred_element_type=f32
        ) + jnp.dot(lefts[left][2][rows], rights[right][1][at, :, chunk], preferred_element_type=f32)
    for copy in copies:
        copy.wait()
    for left, right, at, rows, chunk, out in pieces:
        result = (
            total[:, out]
            + jnp.dot(lefts_in[left][0, rows], rights_in[right][0, at, :, chunk], preferred_element_type=f32)
            + jnp.dot(lefts_in[left][1, rows], rights_in[right][1, at, :, chunk], preferred_element_type=f32)
        )
        keep_ref[:, out] = result[: unit // 2].astype(bf16)
        send_ref[:, out] = result[unit // 2 :].astype(bf16)


def quarter_gradient(lefts, rights, parts, collective, order=()):
    unit = min(left[0].shape[0] for left in lefts)
    columns = sum(
        lefts[left][0].shape[0] // unit * -(-rights[right][0].shape[2] // LANES) * LANES
        for left, right, _ in parts
    )
    vmem = pl.BlockSpec(memory_space=pltpu.VMEM)
    counts = (len(lefts), len(rights))
    inputs = [array for group in lefts + rights for array in group]
    return pl.pallas_call(
        ignoring(functools.partial(quarter_kernel, parts, counts), len(inputs), len(order)),
        in_specs=[vmem] * len(inputs) + [pl.BlockSpec(memory_space=pl.ANY)] * len(order),
        out_specs=[vmem] * 2,
        out_shape=[jax.ShapeDtypeStruct((unit // 2, columns), bf16)] * 2,
        scratch_shapes=[pltpu.VMEM((2,) + left[0].shape, bf16) for left in lefts]
        + [pltpu.VMEM((2,) + right[0].shape, bf16) for right in rights]
        + [
            pltpu.VMEM((unit, columns), f32),
            pltpu.SemaphoreType.DMA((2 * sum(counts),)),
            pltpu.SemaphoreType.DMA((2 * sum(counts),)),
        ],
        compiler_params=pltpu.CompilerParams(
            vmem_limit_bytes=56 * 2**20, collective_id=collective, has_side_effects=True
        ),
        cost_estimate=taking(columns // 320),
        name="gradient",
    )(*inputs, *order)


def added(keep, received):
    total = keep.astype(f32) + received.astype(f32)
    half = total.shape[0] // 2
    return total[:half].astype(bf16), total[half:].astype(bf16)


def shared_rows(right):
    return right, seq_swap(right, 1)


class Gradient:
    def __init__(self, lefts, rights, parts, collective, order=()):
        self.lefts, self.parts, self.collective, self.order = lefts, parts, collective, order
        self.rights = [right if isinstance(right, tuple) else shared_rows(right) for right in rights]
        self.bits = lax.axis_size("seq").bit_length() - 1
        self.bit = 2
        self.total = None

    def start(self):
        self.received = seq_swap(self.send, self.bit)
        self.bit += 1

    def finish(self):
        if self.bit == 2:
            self.keep, self.send = quarter_gradient(
                self.lefts, self.rights, self.parts, self.collective, self.order
            )
        elif self.bit < self.bits:
            self.keep, self.send = added(self.keep, self.received)
        else:
            self.total = self.keep.astype(f32) + self.received.astype(f32)

    def results(self):
        unit = min(left[0].shape[0] for left in self.lefts)
        found, begin = [], 0
        for left, right, _ in self.parts:
            columns = self.rights[right][0].shape[2]
            blocks = []
            for _ in range(self.lefts[left][0].shape[0] // unit):
                blocks.append(self.total[:, begin : begin + columns])
                begin += -(-columns // LANES) * LANES
            found.append(blocks[0] if len(blocks) == 1 else jnp.concatenate(blocks, axis=0))
        return found


def after(value, *others):
    for other in others:
        value = value + (other.reshape(-1)[0] * 0).astype(value.dtype)
    return value


def finished(gradient):
    gradient.finish()
    arrays = [gradient.total] if gradient.total is not None else [gradient.keep, gradient.send]
    if gradient.total is None:
        gradient.start()
    return arrays


def ignoring(body, used, unused):
    return lambda *refs: body(*refs[:used], *refs[used + unused :])


def completed_all(gradients):
    while any(gradient.total is None for gradient in gradients):
        for gradient in gradients:
            if gradient.total is None:
                gradient.finish()
                if gradient.total is None:
                    gradient.start()


def column_chunks(value, chunks):
    width = value.shape[1] // lax.axis_size("wt")
    piece = -(-width // chunks // LANES) * LANES
    owners = cut_evenly(value, 1)
    return [
        to_own_columns(jnp.concatenate([owner[:, at : at + piece] for owner in owners], axis=1))
        for at in range(0, width, piece)
    ]


def lane_blocks(inner):
    blocks = inner // LANES
    return next(n for n in (5, 4, 3, 2, 1) if blocks % n == 0)

def cut_lanes(value):
    return [value[:, i * LANES : (i + 1) * LANES] for i in range(value.shape[1] // LANES)]

def spread(ref, tile, row, states):
    values = ref[tile, row : row + 1, :]
    return [jnp.broadcast_to(part, (states, LANES)) for part in cut_lanes(values)]


def advanced(size_ref, inject_ref, entry_ref, decay, tile, row, state):
    states = entry_ref.shape[1]
    into = entry_ref[tile * 8 + row]
    return tuple(
        jnp.exp2(size * rate) * old + inject * into
        for size, inject, rate, old in zip(
            spread(size_ref, tile, row, states), spread(inject_ref, tile, row, states), decay, state
        )
    )


def no_state(decay_ref):
    return tuple(jnp.zeros_like(part) for part in cut_lanes(decay_ref[...]))


def state_kernel(size_ref, inject_ref, entry_ref, decay_ref, last_ref):
    decay = cut_lanes(decay_ref[...])

    def tokens(tile, state):
        for row in range(8):
            state = advanced(size_ref, inject_ref, entry_ref, decay, tile, row, state)
        return state

    state = lax.fori_loop(0, size_ref.shape[0], tokens, no_state(decay_ref))
    last_ref[...] = jnp.concatenate(state, axis=1)


def output_kernel(size_ref, inject_ref, entry_ref, read_ref, decay_ref, begin_ref, out_ref):
    decay = cut_lanes(decay_ref[...])

    def tokens(tile, state):
        for row in range(8):
            state = advanced(size_ref, inject_ref, entry_ref, decay, tile, row, state)
            output = read_ref[tile * 8 + row]
            for i, part in enumerate(state):
                out_ref[tile, row : row + 1, i * LANES : (i + 1) * LANES] = jnp.sum(
                    output * part, axis=0, keepdims=True
                )
        return state

    lax.fori_loop(0, size_ref.shape[0], tokens, tuple(cut_lanes(begin_ref[...])))


def adjoint_kernel(size_ref, back_ref, read_ref, decay_ref, first_ref):
    states = decay_ref.shape[0]
    decay = cut_lanes(decay_ref[...])
    tiles = size_ref.shape[0]

    def tokens(turn, carry):
        tile = tiles - 1 - turn
        for row in reversed(range(8)):
            output = read_ref[tile * 8 + row]
            carry = tuple(
                jnp.exp2(size * rate) * (output * back + old)
                for size, back, rate, old in zip(
                    spread(size_ref, tile, row, states), spread(back_ref, tile, row, states), decay, carry
                )
            )
        return carry

    carry = lax.fori_loop(0, tiles, tokens, no_state(decay_ref))
    first_ref[...] = jnp.concatenate(carry, axis=1)


def gradient_kernel(
    size_ref,
    inject_ref,
    back_ref,
    entry_ref,
    read_ref,
    decay_ref,
    rate_ref,
    begin_ref,
    end_ref,
    through_ref,
    sized_ref,
    entry_back_ref,
    read_back_ref,
    decay_back_ref,
    prior_ref,
):
    states = decay_ref.shape[0]
    decay = cut_lanes(decay_ref[...])
    tiles = size_ref.shape[0]

    @pl.when(pl.program_id(0) == 0)
    def _():
        entry_back_ref[...] = jnp.zeros_like(entry_back_ref)
        read_back_ref[...] = jnp.zeros_like(read_back_ref)

    def forward(tile, state):
        for row in range(8):
            for i, part in enumerate(state):
                prior_ref[tile * 8 + row, :, i * LANES : (i + 1) * LANES] = part
            state = advanced(size_ref, inject_ref, entry_ref, decay, tile, row, state)
        return state

    last = lax.fori_loop(0, tiles, forward, tuple(cut_lanes(begin_ref[...])))

    def backward(turn, carry):
        tile = tiles - 1 - turn
        arriving, current, total = carry
        for row in reversed(range(8)):
            t = tile * 8 + row
            into = entry_ref[t]
            output = read_ref[t]
            sizes = spread(size_ref, tile, row, states)
            injects = spread(inject_ref, tile, row, states)
            backs = spread(back_ref, tile, row, states)
            entry_back = entry_back_ref[t]
            read_back = read_back_ref[t]
            new_arriving, new_current, new_total = [], [], []
            for k in range(len(decay)):
                lanes = slice(k * LANES, (k + 1) * LANES)
                prior = prior_ref[t, :, lanes]
                adjoint = output * backs[k] + arriving[k]
                leaving = jnp.exp2(sizes[k] * decay[k]) * adjoint
                weighted = leaving * prior
                through_ref[tile, row : row + 1, lanes] = jnp.sum(adjoint * into, axis=0, keepdims=True)
                sized_ref[tile, row : row + 1, lanes] = jnp.sum(
                    weighted * rate_ref[:, lanes], axis=0, keepdims=True
                )
                entry_back = entry_back + adjoint * injects[k]
                read_back = read_back + current[k] * backs[k]
                new_total.append(total[k] + weighted * sizes[k])
                new_arriving.append(leaving)
                new_current.append(prior)
            entry_back_ref[t] = entry_back
            read_back_ref[t] = read_back
            arriving, current, total = new_arriving, new_current, new_total
        return tuple(arriving), tuple(current), tuple(total)

    arriving = tuple(cut_lanes(end_ref[...]))
    _, _, total = lax.fori_loop(0, tiles, backward, (arriving, last, no_state(decay_ref)))
    decay_back_ref[...] = jnp.concatenate(total, axis=1)


def scan_call(body, name, token_args, wide_args, state_args, outs, scratch=False, flops=0, order=()):
    rows, inner = token_args[0].shape
    states = state_args[0].shape[0]
    width = lane_blocks(inner) * LANES
    token = pl.BlockSpec((rows // 8, 8, width), lambda i: (0, 0, i))
    wide = pl.BlockSpec((rows, states, LANES), lambda i: (0, 0, 0))
    state = pl.BlockSpec((states, width), lambda i: (0, i))
    kinds = {
        "token": (token, jax.ShapeDtypeStruct((rows // 8, 8, inner), f32)),
        "wide": (wide, jax.ShapeDtypeStruct((rows, states, LANES), f32)),
        "state": (state, jax.ShapeDtypeStruct((states, inner), f32)),
    }
    size = rows * states * inner
    results = pl.pallas_call(
        ignoring(body, len(token_args) + len(wide_args) + len(state_args), len(order)),
        grid=(inner // width,),
        in_specs=[token] * len(token_args)
        + [wide] * len(wide_args)
        + [state] * len(state_args)
        + [pl.BlockSpec(memory_space=pl.ANY)] * len(order),
        out_specs=[kinds[k][0] for k in outs],
        out_shape=[kinds[k][1] for k in outs],
        scratch_shapes=[pltpu.VMEM((rows, states, width), f32)] if scratch else [],
        compiler_params=pltpu.CompilerParams(vmem_limit_bytes=40 * 2**20),
        cost_estimate=taking(flops * 3 // 2),
        name=name,
    )(*[arg.reshape(rows // 8, 8, inner) for arg in token_args], *wide_args, *state_args, *order)
    return [r.reshape(rows, inner) if k == "token" else r for k, r in zip(outs, results)]


def entering_kernel(sign, hops, total_ref, part_ref, rate_ref, out_ref, totals, parts, totals_in, parts_in, sent, got):
    count = lax.axis_size("seq")
    place = lax.axis_index("seq")
    barrier = pltpu.get_barrier_semaphore()
    reaches = sorted({distance for _, distance in hops})
    for distance in reaches:
        pl.semaphore_signal(
            barrier,
            inc=1,
            device_id={"seq": (place + count - sign * distance) % count},
            device_id_type=pl.DeviceIdType.MESH,
        )
    pl.semaphore_wait(barrier, len(reaches))

    def send(turn):
        buffer, distance = hops[turn]
        copies = [
            pltpu.make_async_remote_copy(
                src_ref=source,
                dst_ref=target,
                send_sem=sent.at[turn, i],
                recv_sem=got.at[turn, i],
                device_id={"seq": (place + count + sign * distance) % count},
                device_id_type=pl.DeviceIdType.MESH,
            )
            for i, (source, target) in enumerate(
                [(totals.at[buffer], totals_in.at[turn]), (parts.at[buffer], parts_in.at[turn])]
            )
        ]
        for copy in copies:
            copy.start()
        return copies

    def joined(near, far):
        (total, part), (far_total, far_part) = near, far
        passed = [
            jnp.exp2(total[k : k + 1] * rate_ref[:, k * LANES : (k + 1) * LANES])
            for k in range(total.shape[0])
        ]
        return total + far_total, jnp.concatenate(passed, axis=1) * far_part + part

    def received(turn, copies):
        for copy in copies:
            copy.wait()
        distance = hops[turn][1]
        there = place >= distance if sign > 0 else place < count - distance
        return jnp.where(there, totals_in[turn], 0.0), jnp.where(there, parts_in[turn].astype(f32), 0.0)

    totals[0] = total_ref[...]
    parts[0] = part_ref[...].astype(bf16)
    first = [send(0), send(1)]
    state = joined(received(0, first[0]), received(1, first[1]))
    for turn in range(2, len(hops)):
        buffer = hops[turn][0]
        totals[buffer] = state[0]
        parts[buffer] = state[1].astype(bf16)
        state = joined(state, received(turn, send(turn)))
    out_ref[...] = state[1]


def entering(total, part, rate, reverse, order):
    count = lax.axis_size("seq")
    states, inner = part.shape
    total = total.reshape(-1, LANES)
    hops = [(0, 1), (0, 2)] + [(bit, 1 << bit) for bit in range(1, count.bit_length() - 1)]
    buffers = len(hops) - 1
    vmem = pl.BlockSpec(memory_space=pltpu.VMEM)
    return pl.pallas_call(
        ignoring(functools.partial(entering_kernel, -1 if reverse else 1, hops), 3, len(order)),
        in_specs=[vmem] * 3 + [pl.BlockSpec(memory_space=pl.ANY)] * len(order),
        out_specs=vmem,
        out_shape=jax.ShapeDtypeStruct(part.shape, f32),
        scratch_shapes=[
            pltpu.VMEM((buffers,) + total.shape, f32),
            pltpu.VMEM((buffers, states, inner), bf16),
            pltpu.VMEM((len(hops),) + total.shape, f32),
            pltpu.VMEM((len(hops), states, inner), bf16),
            pltpu.SemaphoreType.DMA((len(hops), 2)),
            pltpu.SemaphoreType.DMA((len(hops), 2)),
        ],
        compiler_params=pltpu.CompilerParams(
            vmem_limit_bytes=24 * 2**20, collective_id=10 if reverse else 9, has_side_effects=True
        ),
        cost_estimate=taking(24),
        name="entering",
    )(total, part, rate, *order)


def summed_everywhere(values):
    for axis in ("wt", "seq"):
        count = lax.axis_size(axis)
        bit = 1
        while bit < count:
            received = lax.ppermute(values, axis, [(i, i ^ bit) for i in range(count)])
            values = (values.astype(f32) + received.astype(f32)).astype(values.dtype)
            bit *= 2
    return values


def product(left, right):
    return jnp.dot(left, right, preferred_element_type=jnp.float32)


def left_product(left, right):
    return lax.dot_general(
        left, right, (((0,), (0,)), ((), ())), preferred_element_type=jnp.float32
    )


def right_product(left, right):
    return lax.dot_general(
        left, right, (((1,), (1,)), ((), ())), preferred_element_type=jnp.float32
    )


def transposed_dot(left, right):
    return lax.dot_general(left, right, (((0,), (0,)), ((), ())), preferred_element_type=f32)


def heads_beside(value):
    heads = value.shape[0] // HEAD_SIZE
    return jnp.concatenate(
        [value[h * HEAD_SIZE : (h + 1) * HEAD_SIZE] for h in range(heads)], axis=1
    )


def store_heads(ref, value):
    rows = ref.shape[1]
    for h in range(ref.shape[0] // HEAD_SIZE):
        ref[h * HEAD_SIZE : (h + 1) * HEAD_SIZE, :] = value[:, h * rows : (h + 1) * rows].astype(ref.dtype)


def chance_table(query, keys, bias):
    heads = query.shape[1] // bias.shape[1]
    scores = transposed_dot(keys, query) + jnp.concatenate([bias] * heads, axis=1)
    raised = jnp.exp(scores - jnp.max(scores, axis=0, keepdims=True))
    return raised * (1.0 / jnp.sum(raised, axis=0, keepdims=True))


def attend_kernel(query_ref, near_ref, bias_ref, out_ref):
    query = heads_beside(query_ref[...]) * bf16(0.125)
    chances = chance_table(query, near_ref[0], bias_ref[...]).astype(bf16)
    store_heads(out_ref, jnp.dot(near_ref[1], chances, preferred_element_type=f32))


def attend_back_kernel(query_ref, near_ref, back_ref, bias_ref, query_back_ref, kept_ref, sent_ref):
    query = heads_beside(query_ref[...]) * bf16(0.125)
    back = heads_beside(back_ref[...])
    weights = chance_table(query, near_ref[0], bias_ref[...])
    values_back = right_product(back, weights.astype(bf16))
    delta = transposed_dot(near_ref[1], back)
    weighted = weights * delta
    scores_back = (weighted - weights * jnp.sum(weighted, axis=0, keepdims=True)).astype(bf16)
    store_heads(query_back_ref, jnp.dot(near_ref[0], scores_back, preferred_element_type=f32) * 0.125)
    half = kept_ref.shape[2]
    for place, near_back in enumerate((right_product(query, scores_back), values_back)):
        kept_ref[place] = near_back[:, :half]
        sent_ref[place] = near_back[:, half:].astype(bf16)


def attention_call(body, name, wide, near, bias, outs, flops, order=()):
    span, rows = bias.shape
    key_heads = near.shape[1] // HEAD_SIZE
    width = wide[0].shape[0] // key_heads
    wide_spec = pl.BlockSpec((width, rows), lambda k: (k, 0))
    near_spec = lambda size: pl.BlockSpec((2, HEAD_SIZE, size), lambda k: (0, k, 0))
    half = near.shape[:2] + (span // 2,)
    kinds = {
        "wide": (wide_spec, jax.ShapeDtypeStruct(wide[0].shape, bf16)),
        "kept": (near_spec(span // 2), jax.ShapeDtypeStruct(half, f32)),
        "sent": (near_spec(span // 2), jax.ShapeDtypeStruct(half, bf16)),
    }
    return pl.pallas_call(
        ignoring(body, len(wide) + 2, len(order)),
        grid=(key_heads,),
        in_specs=[wide_spec, near_spec(span)]
        + [wide_spec] * (len(wide) - 1)
        + [pl.BlockSpec((span, rows), lambda k: (0, 0))]
        + [pl.BlockSpec(memory_space=pl.ANY)] * len(order),
        out_specs=[kinds[k][0] for k in outs],
        out_shape=[kinds[k][1] for k in outs],
        compiler_params=pltpu.CompilerParams(vmem_limit_bytes=56 * 2**20),
        cost_estimate=taking(flops * 4),
        name=name,
    )(wide[0], near, *wide[1:], bias, *order)


def outer_product(left, right):
    return lax.dot_general(left, right, (((0,), (1,)), ((), ())), preferred_element_type=f32)


def inverse_norm(value):
    return lax.rsqrt(jnp.mean(value * value, axis=-1, keepdims=True) + epsilon)


def norm_back(value, scale, incoming):
    return scale * incoming - scale * scale * scale * value * jnp.mean(
        incoming * value, axis=-1, keepdims=True
    )


def silu_slope(value):
    sigma = jax.nn.sigmoid(value)
    return sigma * (1.0 + value * (1.0 - sigma))


def gather_columns(own):
    count = lax.axis_size("wt")
    turned = own.T
    return in_order([turned] + [from_ahead(turned, k) for k in range(1, count)], 0)


def feed_kernel(
    columns,
    second_ref,
    back_ref,
    gate_ref,
    up_ref,
    down_ref,
    out_ref,
    second_back_ref,
    activated_ref,
    hidden_back_ref,
    out_sum,
    second_back_sum,
):
    width = gate_ref.shape[1]
    step, last = pl.program_id(0), pl.num_programs(0) - 1

    def part(width, begin):
        gate, up, down = (ref[:, :width] for ref in (gate_ref, up_ref, down_ref))
        gate_raw = product(second_ref[...], gate)
        up_raw = product(second_ref[...], up)
        act_back = product(back_ref[...], down)
        sigma = jax.nn.sigmoid(gate_raw)
        swish = gate_raw * sigma
        activated = (swish * up_raw).astype(bf16)
        gate_back = (act_back * up_raw * (sigma * (1.0 + gate_raw * (1.0 - sigma)))).astype(bf16)
        up_back = (act_back * swish).astype(bf16)
        activated_ref[:, :width] = activated
        hidden_back_ref[0, :, :width] = gate_back
        hidden_back_ref[1, :, :width] = up_back
        out = right_product(down, activated)
        second_back = right_product(gate, gate_back) + right_product(up, up_back)
        if begin:
            out_sum[...] = out
            second_back_sum[...] = second_back
        else:
            out_sum[...] += out
            second_back_sum[...] += second_back

    pl.when(step == 0)(lambda: part(width, True))
    pl.when((step > 0) & (step < last))(lambda: part(width, False))

    @pl.when(step == last)
    def _():
        left = columns - (-(-columns // width) - 1) * width
        part(left, False)
        if left < width:
            activated_ref[:, left:] = jnp.zeros((activated_ref.shape[0], width - left), bf16)
            hidden_back_ref[:, :, left:] = jnp.zeros((2, activated_ref.shape[0], width - left), bf16)
        out_ref[...] = out_sum[...].T
        second_back_ref[...] = second_back_sum[...].T


def feed_block(second, back, gate, up, down, order, width=512):
    rows, model = second.shape
    columns = gate.shape[1]
    padded = -(-columns // LANES) * LANES
    whole = pl.BlockSpec((rows, model), lambda i: (0, 0))
    weight = pl.BlockSpec((model, width), lambda i: (0, i))
    hidden = pl.BlockSpec((rows, width), lambda i: (0, i))
    return pl.pallas_call(
        ignoring(functools.partial(feed_kernel, columns), 5, len(order)),
        grid=(-(-columns // width),),
        in_specs=[whole, whole, weight, weight, weight]
        + [pl.BlockSpec(memory_space=pl.ANY)] * len(order),
        out_specs=[whole, whole, hidden, pl.BlockSpec((2, rows, width), lambda i: (0, 0, i))],
        out_shape=[jax.ShapeDtypeStruct((rows, model), f32)] * 2
        + [jax.ShapeDtypeStruct(shape, bf16) for shape in ((rows, padded), (2, rows, padded))],
        scratch_shapes=[pltpu.VMEM((model, rows), f32)] * 2,
        compiler_params=pltpu.CompilerParams(vmem_limit_bytes=48 * 2**20),
        cost_estimate=taking(22),
        name="feed",
    )(second, back, gate, up, down, *order)


def per_device(
    tokens,
    segment_ids,
    cotangent,
    norm_gain,
    query_weight,
    key_weight,
    value_weight,
    head_weight,
    input_weight,
    filter_weight,
    filter_bias,
    select_weight,
    step_weight,
    step_offset,
    decay_log,
    direct_skip_weight,
    mixer_weight,
    attend_gain,
    state_gain,
    feed_gain,
    gate_weight,
    up_weight,
    down_weight,
):
    rows = tokens.shape[1]
    model = tokens.shape[2]
    inner = filter_weight.shape[1]
    kernel = filter_weight.shape[0]
    states = decay_log.shape[0]
    start = lax.axis_index("seq") * rows
    whole_segment = segment_ids[0]
    padded_segment = jnp.concatenate([jnp.full((WINDOW,), -1, jnp.int32), whole_segment])
    segment = lax.dynamic_slice_in_dim(whole_segment, start, rows)
    inputs = tokens[0].astype(jnp.float32)
    upstream = cotangent[0].astype(jnp.float32)
    both_tokens = gather_tokens(tokens[0])
    select_full = gather_columns(select_weight)
    step_full = gather_columns(step_weight)
    rank = step_full.shape[0]
    first_scale = inverse_norm(inputs)
    both_inputs = both_tokens.astype(jnp.float32)
    both_normed = (both_inputs * inverse_norm(both_inputs) * norm_gain).astype(jnp.bfloat16)
    normed_shared = shared_features(both_normed, model)
    pairs = jnp.stack(
        [outer_product(weight, both_normed).astype(bf16) for weight in (key_weight, value_weight)]
    )
    pairs = to_own_tokens(pairs, 2, 1)
    entered = to_own_tokens(product(both_normed, input_weight).astype(jnp.bfloat16))
    both_back = gather_tokens(after(cotangent[0], entered))
    back_shared = shared_features(both_back, model)
    query = to_own_tokens(outer_product(query_weight, both_normed).astype(jnp.bfloat16), 1, 0)
    hops = -(-WINDOW // (4 * rows))
    near = jnp.concatenate(
        [pairs] + [passed_along(pairs, "seq", 4 * hop) for hop in range(1, hops + 1)], axis=2
    )
    seq_place = lax.axis_index("seq")
    block_places = jnp.stack(
        [(seq_place ^ other) - 4 * hop for other in (0, 2, 1, 3) for hop in range(hops + 1)]
    )
    near_place = (block_places[:, None] * rows + jnp.arange(rows, dtype=jnp.int32)[None, :]).reshape(-1)
    near_segment = jnp.where(
        block_places[:, None] >= 0,
        jnp.take(whole_segment.reshape(-1, rows), jnp.maximum(block_places, 0), axis=0),
        -1,
    ).reshape(-1)
    distance = start + jnp.arange(rows, dtype=jnp.int32)[None, :] - near_place[:, None]
    allowed = (distance >= 0) & (distance < WINDOW) & (segment[None, :] == near_segment[:, None])
    bias = jnp.where(allowed, 0.0, masked)
    inner_rows = entered[:, :inner]
    select_full = after(select_full, entered)
    step_full = after(step_full, entered)
    gate_input = entered[:, inner:].astype(jnp.float32)
    before = passed_along(inner_rows[rows - kernel + 1 :], "seq", 1)
    extended = jnp.concatenate([before, inner_rows], axis=0).astype(jnp.float32)
    edge_segment = lax.dynamic_slice_in_dim(
        padded_segment, start + WINDOW - kernel + 1, rows + kernel - 1
    )
    taps = []
    sames = []
    filtered = filter_bias + jnp.zeros((rows, inner), jnp.float32)
    for tap in range(kernel):
        begin = kernel - 1 - tap
        same = (edge_segment[begin : begin + rows] == segment).astype(jnp.float32)
        kept_rows = extended[begin : begin + rows] * same[:, None]
        taps.append(kept_rows)
        sames.append(same)
        filtered = filtered + filter_weight[tap] * kept_rows
    smoothed = (filtered * jax.nn.sigmoid(filtered)).astype(jnp.bfloat16)
    scan_input_rows = smoothed.astype(jnp.float32)
    smoothed_shared = shared_features(smoothed, model)
    projected = right_product(smoothed, select_full)
    step_low = projected[:, :rank].astype(jnp.bfloat16)
    step_low_shared = shared_rows(step_low[None])
    entry = projected[:, rank : rank + states]
    read = projected[:, rank + states :]
    unsquashed_step = product(step_low, step_full) + step_offset
    step = jnp.log1p(jnp.exp(unsquashed_step))
    previous = lax.dynamic_slice_in_dim(padded_segment, start + WINDOW - 1, rows)
    hold = (previous == segment).astype(jnp.float32)
    decay = -jnp.exp(decay_log)
    rate = decay * LOG2E
    size = jnp.where(hold[:, None] == 0.0, 1e30, step)
    inject = step * scan_input_rows
    entry_wide = jnp.broadcast_to(entry[:, :, None], (rows, states, LANES))
    read_wide = jnp.broadcast_to(read[:, :, None], (rows, states, LANES))
    total = jnp.sum(size, axis=0)
    (last,) = scan_call(state_kernel, "scan_state", [size, inject], [entry_wide], [rate], ["state"], flops=4, order=[normed_shared[2]])
    for bit in (1, 0):
        near = jnp.concatenate([near, seq_swap(near, bit)], axis=2)
    (attended,) = attention_call(attend_kernel, "attend", [query], near, bias, ["wide"], 2, order=[back_shared[2]])
    begin_state = entering(total, last, rate, False, [])
    both_attended = gather_tokens(attended, 1)
    attended_shared = shared_features(both_attended, model, turned=False)
    head_out = to_own_tokens(left_product(both_attended, head_weight).astype(bf16)).astype(f32)
    (scanned,) = scan_call(
        output_kernel, "scan_output", [size, inject], [entry_wide, read_wide], [rate, begin_state], ["token"], flops=6, order=[both_back, attended, smoothed_shared[2], step_low_shared[1]]
    )
    scan_result_rows = scanned + direct_skip_weight * scan_input_rows
    sigma_input = jax.nn.sigmoid(gate_input)
    silu_input = gate_input * sigma_input
    gated = (scan_result_rows * silu_input).astype(jnp.bfloat16)
    both_gated = gather_tokens(gated)
    gated_shared = shared_features(both_gated, model)
    branch = to_own_tokens(product(both_gated, mixer_weight).astype(jnp.bfloat16)).astype(f32)
    head_scale = inverse_norm(head_out)
    branch_scale = inverse_norm(branch)
    hidden = inputs + 0.5 * (
        head_out * head_scale * attend_gain + branch * branch_scale * state_gain
    )
    second_scale = inverse_norm(hidden)
    second = (hidden * second_scale * feed_gain).astype(jnp.bfloat16)
    both_second = gather_tokens(second)
    feed_part, second_part, activated, hidden_back = feed_block(
        both_second,
        both_back,
        gate_weight,
        up_weight,
        down_weight,
        [attended_shared[2], gated_shared[2]],
    )
    second_shared = shared_features(both_second, model)
    down = Gradient([back_shared], [activated[None]], [(0, 0, 0)], 1)
    hidden_shared = shared_rows(hidden_back)
    delta_second = summed_tokens(second_part)
    feed_out = summed_tokens(feed_part)
    result = (hidden + feed_out).astype(jnp.bfloat16)
    feed_sum = jnp.sum(delta_second * hidden * second_scale, axis=0)
    delta_hidden = upstream + norm_back(hidden, second_scale, delta_second * feed_gain)
    half = 0.5 * delta_hidden
    attend_sum = jnp.sum(half * head_out * head_scale, axis=0)
    state_sum = jnp.sum(half * branch * branch_scale, axis=0)
    delta_head = norm_back(head_out, head_scale, half * attend_gain).astype(jnp.bfloat16)
    delta_branch = norm_back(branch, branch_scale, half * state_gain).astype(jnp.bfloat16)
    both_deltas = to_own_columns(jnp.stack([delta_head, delta_branch]), 1, 2)
    both_delta_head, both_delta_branch = both_deltas[0], both_deltas[1]
    delta_gated = summed_tokens(right_product(both_delta_branch, mixer_weight))
    delta_attended = summed_tokens(right_product(head_weight, both_delta_head), 1).astype(bf16)
    delta_query, delta_near, sent_near = attention_call(
        attend_back_kernel,
        "attend_back",
        [query, delta_attended],
        near,
        bias,
        ["wide", "kept", "sent"],
        5,
        order=finished(down),
    )
    delta_scan_output = delta_gated * silu_input
    delta_gate = (delta_gated * scan_result_rows * silu_slope(gate_input)).astype(jnp.bfloat16)
    skip_sum = jnp.sum(delta_scan_output * scan_input_rows, axis=0)
    (first,) = scan_call(
        adjoint_kernel,
        "scan_adjoint",
        [size, delta_scan_output],
        [read_wide],
        [rate],
        ["state"],
        flops=4,
        order=[delta_query, hidden_shared[1]],
    )
    end_state = entering(total, first, rate, True, [])
    delta_near = delta_near + seq_swap(sent_near, 0).astype(f32)
    delta_near = after(delta_near, end_state)
    middle = delta_near.shape[2] // 2
    received = seq_swap(delta_near[:, :, middle:].astype(bf16), 1)
    delta_near = delta_near[:, :, :middle] + received.astype(f32)
    delta_pairs = delta_near[:, :, :rows]
    for hop in range(1, hops + 1):
        piece = delta_near[:, :, hop * rows : (hop + 1) * rows].astype(bf16)
        delta_pairs = delta_pairs + passed_along(piece, "seq", -4 * hop).astype(f32)
    delta_pairs = delta_pairs.astype(jnp.bfloat16)
    middle_sums = Gradient(
        [second_shared, attended_shared, gated_shared],
        [hidden_shared, both_deltas],
        [(0, 0, 0), (0, 0, 1), (1, 1, 0), (2, 1, 1)],
        2,
        order=[end_state, delta_pairs],
    )
    through, sized, entry_back, read_back, decay_acc = scan_call(
        gradient_kernel,
        "scan_gradient",
        [size, inject, delta_scan_output],
        [entry_wide, read_wide],
        [rate, decay, begin_state, end_state],
        ["token", "token", "wide", "wide", "state"],
        scratch=True,
        flops=20,
        order=finished(middle_sums),
    )
    both_qkv = jnp.concatenate(
        [
            to_own_columns(delta_query, 1, 0),
            to_own_columns(delta_pairs[0], 1, 0),
            to_own_columns(delta_pairs[1], 1, 0),
        ],
        axis=0,
    ).T
    qkv_shared = shared_rows(both_qkv[None])
    decay_sum = decay_acc * decay
    delta_scan_input = delta_scan_output * direct_skip_weight + through * step
    delta_unsquashed_step = (sized + through * scan_input_rows) * jax.nn.sigmoid(unsquashed_step)
    offset_sum = jnp.sum(delta_unsquashed_step, axis=0)
    raw_low = delta_unsquashed_step.astype(jnp.bfloat16)
    delta_lowrank_step = right_product(raw_low, step_full)
    delta_projected = jnp.concatenate(
        [
            delta_lowrank_step,
            jnp.sum(entry_back, axis=-1),
            jnp.sum(read_back, axis=-1),
        ],
        axis=1,
    ).astype(jnp.bfloat16)
    delta_scan_input = delta_scan_input + product(delta_projected, select_full)
    delta_filtered = delta_scan_input * silu_slope(filtered)
    bias_sum = jnp.sum(delta_filtered, axis=0)
    filter_sums = jnp.stack([jnp.sum(delta_filtered * kept_rows, axis=0) for kept_rows in taps])
    shares = [delta_filtered * filter_weight[tap] * sames[tap][:, None] for tap in range(kernel)]
    leaving = jnp.stack(
        [
            sum(shares[tap][tap - back] for tap in range(back, kernel))
            for back in range(kernel - 1, 0, -1)
        ]
    )
    arrived = passed_along(leaving.astype(jnp.bfloat16), "seq", -1).astype(jnp.float32)
    delta_inner = sum(jnp.pad(share[tap:], ((0, tap), (0, 0))) for tap, share in enumerate(shares))
    delta_inner = delta_inner + jnp.pad(arrived, ((rows - kernel + 1, 0), (0, 0)))
    delta_inner = after(delta_inner, finished(middle_sums)[0])
    delta_entered = jnp.concatenate([delta_inner.astype(jnp.bfloat16), delta_gate], axis=1)
    both_entered = column_chunks(delta_entered, 2)
    widths = (query_weight.shape[1], key_weight.shape[1], value_weight.shape[1])
    cuts = (0, widths[0], widths[0] + widths[1], sum(widths))
    delta_normed = right_product(jnp.concatenate(both_entered, axis=1), input_weight)
    for place, weight in enumerate((query_weight, key_weight, value_weight)):
        delta_normed = delta_normed + right_product(both_qkv[:, cuts[place] : cuts[place + 1]], weight)
    delta_normed = summed_tokens(delta_normed)
    norm_sum = jnp.sum(delta_normed * inputs * first_scale, axis=0)
    delta_tokens = delta_hidden + norm_back(inputs, first_scale, delta_normed * norm_gain)
    raw_shared = shared_features(raw_low, model, order=[both_entered[0]])
    late_sums = Gradient(
        [normed_shared, smoothed_shared, raw_shared],
        [qkv_shared, after(delta_projected, both_entered[0])[None], step_low_shared],
        [(0, 0, 0), (1, 1, 0), (2, 2, 0)],
        3,
        order=[both_entered[0]],
    )
    middle_placed = finished(middle_sums)
    input_sums = [
        Gradient([normed_shared], [part[None]], [(0, 0, 0)], 4 if part.shape == both_entered[0].shape else 5, middle_placed)
        for part in both_entered
    ]
    for gradient in input_sums:
        finished(gradient)
    input_placed = input_sums[-1].keep
    completed_all(input_sums + [late_sums, down, middle_sums])
    qkv_gradient, select_sum, step_sum = late_sums.results()
    query_gradient, key_gradient, value_gradient = (
        qkv_gradient[:, cuts[place] : cuts[place + 1]] for place in range(3)
    )
    select_gradient, step_gradient = own_columns_sums((select_sum, step_sum))
    input_gradient = jnp.concatenate([gradient.results()[0] for gradient in input_sums], axis=1)
    gate_gradient, up_gradient, head_gradient, mixer_gradient = middle_sums.results()
    (down_gradient,) = down.results()
    hidden_width = gate_weight.shape[1]
    gate_gradient, up_gradient, down_gradient = (
        gradient[:, :hidden_width] for gradient in (gate_gradient, up_gradient, down_gradient)
    )
    early = jnp.concatenate(
        [
            decay_sum,
            filter_sums,
            jnp.stack([bias_sum, offset_sum, skip_sum, jnp.concatenate([attend_sum, state_sum])]),
            jnp.concatenate([feed_sum, norm_sum])[None],
        ],
        axis=0,
    )
    early_total = summed_everywhere(after(early, input_placed).astype(bf16)).astype(f32)
    decay_total = early_total[:states]
    filter_total = early_total[states : states + kernel]
    bias_total, offset_total, skip_total, pair_total, last_total = early_total[states + kernel :]
    attend_total, state_total = pair_total[:model], pair_total[model:]
    feed_total, norm_total = last_total[:model], last_total[model:]
    return (
        result[None],
        delta_tokens[None],
        norm_total,
        query_gradient,
        key_gradient,
        value_gradient,
        head_gradient,
        input_gradient,
        filter_total,
        bias_total,
        select_gradient,
        step_gradient,
        offset_total,
        decay_total,
        skip_total,
        mixer_gradient,
        attend_total,
        state_total,
        feed_total,
        gate_gradient,
        up_gradient,
        down_gradient,
    )


def solution(mesh):
    placed = (
        P("wt", "seq", None),
        P("wt", None),
        P("wt", "seq", None),
        P(),
        P(None, "wt"),
        P(None, "wt"),
        P(None, "wt"),
        P(None, "wt"),
        P(None, "wt"),
        P(),
        P(),
        P(None, "wt"),
        P(None, "wt"),
        P(),
        P(),
        P(),
        P(None, "wt"),
        P(),
        P(),
        P(),
        P(None, "wt"),
        P(None, "wt"),
        P(None, "wt"),
    )
    return jax.shard_map(
        per_device,
        mesh=mesh,
        in_specs=placed,
        out_specs=(
            P("wt", "seq", None),
            P("wt", "seq", None),
            P(),
            P("seq", "wt"),
            P("seq", "wt"),
            P("seq", "wt"),
            P("seq", "wt"),
            P("seq", "wt"),
            P(),
            P(),
            P("seq", "wt"),
            P("seq", "wt"),
            P(),
            P(),
            P(),
            P("seq", "wt"),
            P(),
            P(),
            P(),
            P("seq", "wt"),
            P("seq", "wt"),
            P("seq", "wt"),
        ),
        check_vma=False,
    )
```
